128 devices in a mesh: ctx: 8 (over x, core), tp: 16 (over y, z).
Axes of the slice: x: 4, y: 4, z: 4, core: 2. Of those that a mesh axis runs over, the one named last changes fastest.
Arguments:
- mamba_in: bfloat16 [8192, 16384], P(('ctx', 'tp')), may hold values from -6 to 6
- state_in_b: float32 [8192, 16], P('ctx'), may hold values from -6 to 6
- state_out_c: float32 [8192, 16], P('ctx'), may hold values from -1.5 to 1.5
- step_decay: float32 [8192, 256], P('ctx', 'tp'), may hold values from -1 to 0, as said below
- skip_gain: float32 [256], P('tp'), may hold values from 0.5 to 1.5
- queries: bfloat16 [8192, 8192], P(('ctx', 'tp')), may hold values from -6 to 6
- keys: bfloat16 [8192, 1024], P(('ctx', 'tp')), may hold values from -6 to 6
- values: bfloat16 [8192, 1024], P(('ctx', 'tp')), may hold values from -6 to 6
- doc_ids: int32 [64], replicated, may hold values from 0 to 3, never falling along the last dimension, each value on 1 to 40 neighbouring positions
Outputs:
- mamba_out: bfloat16 [8192, 16384], P(('ctx', 'tp'))
- attn_out: bfloat16 [8192, 8192], P(('ctx', 'tp'))
The draws below stay inside these ranges and needn't reach their ends.
Inputs may be any that keep to these rules, and one draw needn't show every extreme that they name: `step_decay`: strictly negative.
All inputs are finite; a program needn't handle non-finite values.
Results may differ from the reference program's by a relative error of at most 0.008.
Values may be sent and summed in bfloat16 or wider, within the bound.
No kernel may reach another device: no remote copies, remote signals or barrier semaphores. Data moves between devices by JAX's collectives and lax.ppermute only.
A program may use at most 128 MiB of HBM per device.

```python
import math
import jax
import jax.numpy as jnp
import numpy as np
from jax import lax

DI = 16384
NS = 16
QH = 64
KVH = 8
HD = 128
P_SIZE = 64
SPAN = 128
BLK = 128
TOK_DEV = 1024
HM = 256
SEQUENCE_TOKENS = 8192
NBLK = 64
N_CTX = 8


def draw_queries(key, part):
    key = jax.random.fold_in(key, 101)
    base = jnp.clip(jax.random.normal(key, (SEQUENCE_TOKENS, QH * HD), jnp.float32), -6.0, 6.0)
    return base.astype(jnp.bfloat16)


def draw_keys(key, part):
    key = jax.random.fold_in(key, 202)
    base = jnp.clip(jax.random.normal(key, (SEQUENCE_TOKENS, KVH * HD), jnp.float32), -6.0, 6.0)
    return base.astype(jnp.bfloat16)


def draw_step_decay(key, part):
    key = jax.random.fold_in(key, 303)
    slow_share = 0.5
    is_slow = jax.random.uniform(jax.random.fold_in(key, 1), (HM,)) < slow_share
    fast_rate = jnp.exp(jax.random.uniform(jax.random.fold_in(key, 2), (HM,), jnp.float32, math.log(1.0 / 50.0), math.log(1.0 / 30.0)))
    slow_rate = jnp.exp(jax.random.uniform(jax.random.fold_in(key, 3), (HM,), jnp.float32, math.log(0.3), math.log(0.8))) / SEQUENCE_TOKENS
    decay_speed = jnp.where(is_slow, slow_rate, fast_rate)
    block_factor = jnp.exp(jax.random.uniform(jax.random.fold_in(key, 4), (NBLK, HM), jnp.float32, -math.log(2.0), math.log(2.0)))
    row_multiplier = jnp.repeat(block_factor, BLK, axis=0)
    approximate_estimate = jax.random.uniform(jax.random.fold_in(key, 5), (SEQUENCE_TOKENS, HM), jnp.float32, 0.5, 1.5)
    group_run_rows = jax.random.randint(jax.random.fold_in(key, 6), (3,), 0, SEQUENCE_TOKENS)
    group_run_length = jax.random.uniform(jax.random.fold_in(key, 7), (3,), jnp.float32, 0.22, 0.51)
    token_group_run = jnp.zeros((SEQUENCE_TOKENS,), jnp.float32).at[group_run_rows].set(group_run_length)
    return -(decay_speed[None, :] * row_multiplier * approximate_estimate) - token_group_run[:, None]


def block_levels(key, shape, split, low, largest):
    factor_of, own = 1.0, jax.random.fold_in(key, 6)
    for dim, shards_of in split:
        heights = jnp.exp(jax.random.uniform(jax.random.fold_in(own, dim), (shards_of,), jnp.float32, low / len(split), largest / len(split)))
        factor_of = factor_of * jnp.repeat(heights, shape[dim] // shards_of).reshape([-1 if axis == dim else 1 for axis in range(len(shape))])
    return factor_of


def split_up(amount, total, bound, slope):
    loads = [(1 << 20) // math.isqrt(grade ** slope) + 1 for grade in range(2, amount + 1)]
    surplus, given = total - bound - (amount - 1), [1] * (amount - 1)
    while surplus > 0:
        candidates = [i for i in range(amount - 1) if given[i] < bound]
        pool, remaining = sum([loads[i] for i in candidates]), surplus
        for i in candidates:
            addition = min(bound - given[i], max(1, remaining * loads[i] // pool), surplus)
            given[i] = given[i] + addition
            surplus = surplus - addition
    return np.array([bound] + given)


def ragged(rng, amount, total, reach, lean):
    if amount == 2:
        one = jax.random.randint(rng, (), max(1, total - reach), min(reach, total - 1) + 1)
        return jnp.stack([one, total - one])
    tallies = jnp.asarray(split_up(amount, total, reach, lean), jnp.int32)
    couples = (amount - 1) // 2
    donor, sink = tallies[1:1 + 2 * couples:2], tallies[2:2 + 2 * couples:2]
    margin = jnp.minimum(donor - 1, reach - sink)
    moved = jax.random.randint(jax.random.fold_in(rng, 1), (couples,), 0, 1 << 20) % (margin + 1)
    tallies = tallies.at[1:1 + 2 * couples:2].set(donor - moved).at[2:2 + 2 * couples:2].set(sink + moved)
    return tallies[jax.random.permutation(jax.random.fold_in(rng, 2), amount)]


def bell_draw(own_key, extent, scale, reach, shards=(), held_as=jnp.bfloat16):
    level = block_levels(own_key, extent, shards, -0.22, 0.18) if shards else 1.0
    values = jax.random.normal(own_key, extent, jnp.float32) * scale * level
    return jnp.minimum(jnp.maximum(values, -reach), reach).astype(held_as)


def setup_inputs(seed: int = 0) -> dict:
    streams_of = jax.random.split(jax.random.key(seed), 10)
    return {
        "mamba_in": bell_draw(streams_of[0], (SEQUENCE_TOKENS, DI), 1.0, 6.0, ((0, 128),)),
        "state_in_b": bell_draw(streams_of[1], (SEQUENCE_TOKENS, NS), 1.0, 6.0, ((0, 8),), jnp.float32),
        "state_out_c": bell_draw(streams_of[2], (SEQUENCE_TOKENS, NS), 0.25, 1.5, ((0, 8),), jnp.float32),
        "step_decay": draw_step_decay(jax.random.fold_in(streams_of[9], 71), 0),
        "skip_gain": jnp.clip(1.0 + 0.1 * jax.random.normal(streams_of[4], (HM,), jnp.float32), 0.5, 1.5),
        "queries": draw_queries(jax.random.fold_in(streams_of[9], 71), 0),
        "keys": draw_keys(jax.random.fold_in(streams_of[9], 71), 0),
        "values": bell_draw(streams_of[7], (SEQUENCE_TOKENS, KVH * HD), 1.0, 6.0, ((0, 128),)),
        "doc_ids": jnp.searchsorted(jnp.cumsum(ragged(streams_of[8], 4, NBLK, 5 * NBLK // 8, 0)), jnp.arange(NBLK), side="right").astype(jnp.int32),
    }


NEG_FILL = -1e+30
HIGHEST = lax.Precision.HIGHEST

def ssd_blocks(inputs, decay, state_in_b, state_out_c, initial, span_len):
    row_count, head_count, head_width = inputs.shape
    span_count = row_count // span_len
    inject = jnp.sqrt(-jnp.expm1(2.0 * decay))
    driven = (inputs * inject[:, :, None]).reshape(span_count, span_len, head_count, head_width)
    running = jnp.cumsum(decay.reshape(span_count, span_len, head_count), axis=1)
    b_blocks = state_in_b.reshape(span_count, span_len, -1)
    c_blocks = state_out_c.reshape(span_count, span_len, -1)
    causal_tri = jnp.tril(jnp.ones((span_len, span_len), dtype=bool))

    def advance(state_now, members):
        driven_c, running_c, b_span, c_span = members
        spread = running_c[:, None, :] - running_c[None, :, :]
        within = jnp.exp(jnp.where(causal_tri[:, :, None], spread, NEG_FILL))
        intersection = jnp.dot(c_span, b_span.T, precision=HIGHEST)
        inside = jnp.einsum('tsh,shp->thp', within * intersection[:, :, None], driven_c, precision=HIGHEST)
        entering = jnp.einsum('tn,hpn->thp', c_span, state_now, precision=HIGHEST) * jnp.exp(running_c)[:, :, None]
        remain = jnp.exp(running_c[-1][None, :] - running_c)
        state_next = state_now * jnp.exp(running_c[-1])[:, None, None] + jnp.einsum('shp,sn->hpn', driven_c * remain[:, :, None], b_span, precision=HIGHEST)
        return (state_next, inside + entering)
    final_state, outputs = lax.scan(advance, initial, (driven, running, b_blocks, c_blocks))
    return (outputs.reshape(row_count, head_count, head_width), final_state)

def reference(mamba_in, state_in_b, state_out_c, step_decay, skip_gain, queries, keys, values, doc_ids):
    inputs = mamba_in.astype(jnp.float32).reshape(SEQUENCE_TOKENS, HM, P_SIZE)
    initial = jnp.zeros((HM, P_SIZE, NS), jnp.float32)
    outputs, final_state = ssd_blocks(inputs, step_decay, state_in_b, state_out_c, initial, SPAN)
    mamba_out = (outputs + skip_gain[None, :, None] * inputs).reshape(SEQUENCE_TOKENS, DI).astype(jnp.bfloat16)
    score_scale = HD ** (-0.5)
    group_size = QH // KVH
    position = jnp.arange(SEQUENCE_TOKENS, dtype=jnp.int32)
    row_doc = doc_ids[position // BLK]
    query_groups = queries.reshape(SEQUENCE_TOKENS, KVH, group_size, HD)
    key_groups = keys.reshape(SEQUENCE_TOKENS, KVH, HD)
    value_groups = values.reshape(SEQUENCE_TOKENS, KVH, HD)
    pieces = []
    for block_index in range(N_CTX):
        low_row = block_index * TOK_DEV
        high_row = low_row + TOK_DEV
        visible = (row_doc[low_row:high_row, None] == row_doc[None, :high_row]) & (position[low_row:high_row, None] >= position[None, :high_row])

        def one_group(members):
            query_part, key_part, value_part = members
            scores = jnp.einsum('tgd,kd->gtk', query_part.astype(jnp.float32), key_part.astype(jnp.float32)) * score_scale
            scores = jnp.where(visible[None], scores, NEG_FILL)
            top_score = lax.optimization_barrier(jnp.max(scores, axis=-1, keepdims=True))
            terms = jnp.where(visible[None], jnp.exp(scores - top_score), 0.0)
            totals = lax.optimization_barrier(jnp.sum(terms, axis=-1))
            weights = terms.astype(jnp.bfloat16)
            context = jnp.einsum('gtk,kd->gtd', weights.astype(jnp.float32), value_part.astype(jnp.float32))
            return context / totals[:, :, None]
        result = lax.map(one_group, (jnp.transpose(query_groups[low_row:high_row], (1, 0, 2, 3)), jnp.transpose(key_groups[:high_row], (1, 0, 2)), jnp.transpose(value_groups[:high_row], (1, 0, 2))))
        pieces.append(jnp.transpose(result, (2, 0, 1, 3)).reshape(TOK_DEV, QH * HD))
    attn_out = jnp.concatenate(pieces, axis=0).astype(jnp.bfloat16)
    return (mamba_out, attn_out)
```

```python
import math

import jax
import jax.numpy as jnp
from jax import lax
from jax.experimental import pallas as pl
from jax.experimental.pallas import tpu as pltpu
from jax.sharding import Mesh, PartitionSpec as P

NS = 16
KVH = 8
HD = 128
HM = 256
CHUNK = 64
NEG = -1e30
SCORE_EXP2 = HD**-0.5 * math.log2(math.e)
HIGHEST = lax.Precision.HIGHEST
F32 = jnp.float32
BF16 = jnp.bfloat16
ALL = ("x", "core", "y", "zh", "zl")
CTX = ("x", "core")
TP = ("y", "zh", "zl")
HEADS = ("x", "zh")
SHARE = ("core", "y", "zl")
VMEM = pl.BlockSpec(memory_space=pltpu.VMEM)
SMEM = pl.BlockSpec(memory_space=pltpu.SMEM)
TK = 1024
NG = 2
RG = 512 // NG


def dot(a, b, dims=((1,), (0,)), precision=None):
    return lax.dot_general(
        a, b, (dims, ((), ())), precision=precision, preferred_element_type=F32
    )


def params(mib):
    return pltpu.CompilerParams(vmem_limit_bytes=mib * 1024 * 1024)


def attn_kernel(meta_ref, q_ref, kv_ref, o_ref, m_ref, acc_ref, s_ref, vt_ref):
    def key_tile(j, low):
        x, core = j // 2, j % 2
        parts = [
            kv_ref[core, y, zl, x, zh, :, low : low + HD]
            for y in range(4)
            for zh in range(2)
            for zl in range(2)
        ]
        return jnp.concatenate(parts, axis=0)

    @pl.loop(0, vt_ref.shape[0])
    def _(j):
        vt_ref[j, :HD, :] = key_tile(j, HD).T
        vt_ref[j, HD:, :] = jnp.ones((16, TK), BF16)

    def scores(i, j, slot):
        k = key_tile(j, 0)
        for g in range(NG):
            s_ref[slot, g] = dot(k, q_ref[i, g * RG : (g + 1) * RG, :], ((1,), (1,)))

    def absorb(i, j, slot, masked):
        v = vt_ref[j]
        if masked:
            kpos = j * TK + lax.broadcasted_iota(jnp.int32, (TK, RG), 0)
            qpos = meta_ref[0, i] + lax.broadcasted_iota(jnp.int32, (TK, RG), 1) % CHUNK
            visible = (kpos <= qpos) & (kpos >= meta_ref[1, i])
        for g in range(NG):
            s = s_ref[slot, g]
            if masked:
                s = jnp.where(visible, s, NEG)
            before = m_ref[g]
            top = jnp.maximum(before, jnp.max(s, axis=0, keepdims=True))
            p = jnp.exp2((s - top) * SCORE_EXP2)
            fade = jnp.exp2((before - top) * SCORE_EXP2)
            m_ref[g] = top
            acc_ref[g] = acc_ref[g] * fade + dot(v, p.astype(BF16))

    def reset():
        m_ref[...] = jnp.full_like(m_ref, NEG)
        acc_ref[...] = jnp.zeros_like(acc_ref)

    def body(carry):
        i, j, slot = carry
        first = meta_ref[1, i]
        last = j == meta_ref[0, i] // TK
        i_next = jnp.where(last, i + 1, i)
        i_read = jnp.minimum(i_next, 7)
        j_next = jnp.where(last, meta_ref[1, i_read] // TK, j + 1)
        edge = last | (j * TK < first)

        @pl.when(edge)
        def _():
            scores(i_read, j_next, 1 - slot)
            absorb(i, j, slot, True)

        @pl.when(jnp.logical_not(edge))
        def _():
            scores(i_read, j_next, 1 - slot)
            absorb(i, j, slot, False)

        @pl.when(last)
        def _():
            for g in range(NG):
                out = (acc_ref[g, :HD] * (1.0 / acc_ref[g, HD : HD + 1])).T
                o_ref[i, g * RG : (g + 1) * RG] = out.astype(BF16)
            reset()

        return (i_next, j_next, 1 - slot)

    reset()
    scores(0, meta_ref[1, 0] // TK, 0)
    lax.while_loop(
        lambda carry: carry[0] < 8, body, (jnp.int32(0), meta_ref[1, 0] // TK, jnp.int32(0))
    )


def attend(meta, q, kv):
    return pl.pallas_call(
        attn_kernel,
        out_shape=jax.ShapeDtypeStruct((8, 512, HD), BF16),
        in_specs=[SMEM, VMEM, VMEM],
        out_specs=VMEM,
        scratch_shapes=[
            pltpu.VMEM((NG, 1, RG), F32),
            pltpu.VMEM((NG, HD + 16, RG), F32),
            pltpu.VMEM((2, NG, TK, RG), F32),
            pltpu.VMEM((8192 // TK, HD + 16, TK), BF16),
        ],
        compiler_params=params(40),
        cost_estimate=pl.CostEstimate(
            flops=4 * 512 * HD * 20000, bytes_accessed=6 << 20, transcendentals=10_000_000
        ),
    )(meta, q, kv)


def one_minus_exp(u):
    small = -u * (
        1
        + u / 2 * (1 + u / 3 * (1 + u / 4 * (1 + u / 5 * (1 + u / 6 * (1 + u / 7 * (1 + u / 8))))))
    )
    return jnp.where(u > -0.5, small, 1 - jnp.exp(u))


def spread(columns, heads, lanes=CHUNK):
    rows = columns.shape[0]
    left = lax.broadcasted_iota(jnp.int32, (rows, 2 * lanes), 1) < lanes
    parts = []
    for h in range(0, heads, 2):
        a = jnp.broadcast_to(columns[:, h : h + 1], (rows, 2 * lanes))
        b = jnp.broadcast_to(columns[:, h + 1 : h + 2], (rows, 2 * lanes))
        parts.append(jnp.where(left, a, b))
    return jnp.concatenate(parts, axis=1)


def running_decay(decay):
    row = lax.broadcasted_iota(jnp.int32, (CHUNK, CHUNK), 0)
    col = lax.broadcasted_iota(jnp.int32, (CHUNK, CHUNK), 1)
    tri = jnp.where(row >= col, 1.0, 0.0).astype(F32)
    return dot(tri, decay, precision=HIGHEST)


def state_kernel(x_ref, dec_ref, b_ref, s_ref, f_ref, e_ref):
    decay = dec_ref[...].T[:CHUNK]
    run = running_decay(decay)
    drive = jnp.exp(-run) * jnp.sqrt(one_minus_exp(2.0 * decay))
    end = jnp.exp(run[CHUNK - 1 :])
    for k in range(16):
        f_ref[k, :, :16] = drive[:, 16 * k : 16 * k + 16]
        e_ref[k, :, :16] = jnp.broadcast_to(end[:, 16 * k : 16 * k + 16], (16, 16))
    b = b_ref[...]
    b_high = b.astype(BF16)
    b_low = (b - b_high.astype(F32)).astype(BF16)
    b_two = jnp.concatenate([b_high, b_low], axis=1)

    @pl.loop(0, 16)
    def _(k):
        cols = pl.ds(pl.multiple_of(k * 1024, 1024), 1024)
        z = (x_ref[:, cols].astype(F32) * spread(f_ref[k], 16)).astype(BF16)
        two = dot(b_two, z, ((0,), (0,)))
        s_ref[k] = ((two[:NS] + two[NS:]) * spread(e_ref[k], 16)).astype(BF16)


def chunk_states(x, dec, b):
    return pl.pallas_call(
        state_kernel,
        out_shape=jax.ShapeDtypeStruct((16, NS, 1024), BF16),
        in_specs=[VMEM] * 3,
        out_specs=VMEM,
        scratch_shapes=[pltpu.VMEM((16, CHUNK, 128), F32), pltpu.VMEM((16, 16, 128), F32)],
        compiler_params=params(16),
        cost_estimate=pl.CostEstimate(
            flops=2 * 32 * CHUNK * 16384, bytes_accessed=3 << 20, transcendentals=50_000
        ),
    )(x, dec, b)


def output_kernel(x_ref, dec_ref, b_ref, c_ref, e_ref, y_ref, f_ref, r_ref, g_ref):
    both = dec_ref[...].T
    decay = both[:CHUNK]
    run = running_decay(decay)
    drive = jnp.exp(-run) * jnp.sqrt(one_minus_exp(2.0 * decay))
    reach = jnp.exp(run)
    gain = jnp.broadcast_to(both[CHUNK : CHUNK + 1], (8, HM))
    for k in range(16):
        f_ref[k, :, :16] = drive[:, 16 * k : 16 * k + 16]
        r_ref[k, :, :16] = reach[:, 16 * k : 16 * k + 16]
        g_ref[k, :, :16] = gain[:, 16 * k : 16 * k + 16]
    row = lax.broadcasted_iota(jnp.int32, (CHUNK, CHUNK), 0)
    col = lax.broadcasted_iota(jnp.int32, (CHUNK, CHUNK), 1)
    inner = jnp.where(row >= col, dot(c_ref[...], b_ref[...], ((1,), (1,)), HIGHEST), 0.0)
    weights = jnp.concatenate([inner, c_ref[...]], axis=1).astype(BF16)

    @pl.loop(0, 16)
    def _(k):
        cols = pl.ds(pl.multiple_of(k * 1024, 1024), 1024)
        x = x_ref[:, cols].astype(F32)
        z = (x * spread(f_ref[k], 16)).astype(BF16)
        y = dot(weights, jnp.concatenate([z, e_ref[k]], axis=0))
        y = y * spread(r_ref[k], 16) + spread(g_ref[k], 16)[:1] * x
        y_ref[:, cols] = y.astype(BF16)


def chunk_outputs(x, dec, b, c, entering):
    return pl.pallas_call(
        output_kernel,
        out_shape=jax.ShapeDtypeStruct((CHUNK, 16384), BF16),
        in_specs=[VMEM] * 5,
        out_specs=VMEM,
        scratch_shapes=[
            pltpu.VMEM((16, CHUNK, 128), F32),
            pltpu.VMEM((16, CHUNK, 128), F32),
            pltpu.VMEM((16, 8, 128), F32),
        ],
        compiler_params=params(24),
        cost_estimate=pl.CostEstimate(
            flops=2 * 80 * CHUNK * 16384, bytes_accessed=5 << 20, transcendentals=50_000
        ),
    )(x, dec, b, c, entering)


def chunk_decays(own_ref, d_ref):
    token = lax.broadcasted_iota(jnp.int32, (1024, 16), 0)
    chunk = lax.broadcasted_iota(jnp.int32, (1024, 16), 1)
    pick = jnp.where(token // CHUNK == chunk, 1.0, 0.0).astype(F32)
    total = dot(pick, own_ref[...], ((0,), (1,)), HIGHEST)
    d_ref[...] = spread(jnp.exp(total), 16)
    return spread(jnp.exp(jnp.sum(total, axis=0, keepdims=True)), 16)


def ends_kernel(s_ref, own_ref, end_ref, d_ref):
    through = chunk_decays(own_ref, d_ref)
    state = jnp.zeros((NS, 1024), F32)
    for k in range(16):
        state = state * d_ref[k : k + 1] + s_ref[k].astype(F32)
    high = through.astype(BF16).astype(F32)
    row = lax.broadcasted_iota(jnp.int32, (16, 1024), 0)
    tail = jnp.where(row == 0, high, jnp.where(row == 1, through - high, 0.0))
    end_ref[...] = jnp.concatenate([state, tail], axis=0).astype(BF16)


def local_ends(states, own):
    return pl.pallas_call(
        ends_kernel,
        out_shape=jax.ShapeDtypeStruct((32, 1024), BF16),
        in_specs=[VMEM] * 2,
        out_specs=VMEM,
        scratch_shapes=[pltpu.VMEM((16, 1024), F32)],
        compiler_params=params(8),
    )(states, own)


def enter_kernel(place_ref, s_ref, own_ref, ends_ref, e_ref, d_ref):
    chunk_decays(own_ref, d_ref)
    place = place_ref[0]
    state = jnp.zeros((NS, 1024), F32)
    for c in range(7):
        through = (ends_ref[c, 16:17].astype(F32) + ends_ref[c, 17:18].astype(F32))
        later = state * through + ends_ref[c, :16].astype(F32)
        state = jnp.where(c < place, later, state)
    for k in range(16):
        e_ref[k] = state.astype(BF16)
        state = state * d_ref[k : k + 1] + s_ref[k].astype(F32)


def entering_states(place, states, own, ends):
    return pl.pallas_call(
        enter_kernel,
        out_shape=jax.ShapeDtypeStruct((16, NS, 1024), BF16),
        in_specs=[SMEM, VMEM, VMEM, VMEM],
        out_specs=VMEM,
        scratch_shapes=[pltpu.VMEM((16, 1024), F32)],
        compiler_params=params(8),
    )(place, states, own, ends)


def per_device(
    mamba_in, state_in_b, state_out_c, step_decay, skip_gain, queries, keys, values, doc_ids
):
    core, y, zl = lax.axis_index("core"), lax.axis_index("y"), lax.axis_index("zl")
    ctx, tp = lax.axis_index(CTX), lax.axis_index(TP)

    kv = jnp.concatenate([keys.reshape(CHUNK, KVH, HD), values.reshape(CHUNK, KVH, HD)], axis=2)
    kv = lax.all_to_all(kv.transpose(1, 0, 2), HEADS, 0, 0, tiled=True)
    kv = lax.all_gather(kv, SHARE).reshape(2, 4, 2, 4, 2, CHUNK, 2 * HD)

    own = step_decay.T
    dec = own.reshape(16, 16, CHUNK).transpose(1, 0, 2)
    gain = jnp.broadcast_to(skip_gain[None, :, None], (16, 16, CHUNK))
    dec = lax.all_to_all(jnp.concatenate([dec, gain], axis=2), TP, 0, 0, tiled=True)
    dec = dec.reshape(HM, 2 * CHUNK)
    b = lax.dynamic_slice_in_dim(state_in_b, tp * CHUNK, CHUNK, 0)
    c = lax.dynamic_slice_in_dim(state_out_c, tp * CHUNK, CHUNK, 0)

    states = chunk_states(mamba_in, dec, b)
    states = lax.all_to_all(states, TP, 0, 0, tiled=True)
    ends = lax.all_gather(local_ends(states, own), CTX)
    entering = entering_states(ctx.reshape(1).astype(jnp.int32), states, own, ends)
    entering = lax.all_to_all(entering, TP, 0, 0, tiled=True)
    mamba_out = chunk_outputs(mamba_in, dec, b, c, entering)

    q = queries.reshape(CHUNK, KVH, 8, HD).transpose(1, 2, 0, 3)
    q = lax.all_to_all(q, HEADS, 0, 0, tiled=True).reshape(8, 512, HD)
    source = jnp.arange(8, dtype=jnp.int32)
    place = (2 * (source // 2) + core) * 1024 + (4 * y + 2 * (source % 2) + zl) * CHUNK
    block = jnp.arange(64, dtype=jnp.int32)
    doc = jnp.sum(jnp.where(block[None] == place[:, None] // 128, doc_ids[None], 0), axis=1)
    first = jnp.sum((doc_ids[None] < doc[:, None]).astype(jnp.int32), axis=1) * 128
    attn = attend(jnp.stack([place, first]).astype(jnp.int32), q, kv)
    attn = lax.all_to_all(attn.reshape(8, 8, CHUNK, HD), HEADS, 0, 0, tiled=True)
    attn_out = attn.transpose(2, 0, 1, 3).reshape(CHUNK, -1)
    return (mamba_out, attn_out)


def solution(mesh):
    inner = Mesh(mesh.devices.reshape(4, 2, 4, 2, 2), ALL)
    in_specs = (
        P(ALL, None),
        P(CTX, None),
        P(CTX, None),
        P(CTX, TP),
        P(TP),
        P(ALL, None),
        P(ALL, None),
        P(ALL, None),
        P(),
    )
    out_specs = (P(ALL, None), P(ALL, None))
    return jax.shard_map(
        per_device, mesh=inner, in_specs=in_specs, out_specs=out_specs, check_vma=False
    )
```

```python
import math

import jax
import jax.numpy as jnp
from jax import lax
from jax.experimental import pallas as pl
from jax.experimental.pallas import tpu as pltpu
from jax.sharding import Mesh, PartitionSpec as P

NS = 16
KVH = 8
HD = 128
HM = 256
CHUNK = 64
NEG = -1e30
SCORE_EXP2 = HD**-0.5 * math.log2(math.e)
HIGHEST = lax.Precision.HIGHEST
F32 = jnp.float32
BF16 = jnp.bfloat16
ALL = ("x", "core", "y", "zh", "zl")
CTX = ("x", "core")
TP = ("y", "zh", "zl")
HEADS = ("x", "zh")
VMEM = pl.BlockSpec(memory_space=pltpu.VMEM)
SMEM = pl.BlockSpec(memory_space=pltpu.SMEM)
ANY = pl.BlockSpec(memory_space=pl.ANY)
TK = 1024
NG = 4
RG = 1024 // NG
SMALL = pltpu.CompilerParams(vmem_limit_bytes=16 << 20)


def dot(a, b, dims=((1,), (0,)), precision=None):
    return lax.dot_general(
        a, b, (dims, ((), ())), precision=precision, preferred_element_type=F32
    )


def split_kernel(q_ref, k_ref, v_ref, o_ref):
    for h in range(KVH):
        o_ref[h, :, :1024] = q_ref[:, h * 1024 : (h + 1) * 1024]
        o_ref[h, :, 1024 : 1024 + HD] = k_ref[:, h * HD : (h + 1) * HD]
        o_ref[h, :, 1024 + HD :] = v_ref[:, h * HD : (h + 1) * HD]


def split_heads(queries, keys, values):
    return pl.pallas_call(
        split_kernel,
        out_shape=jax.ShapeDtypeStruct((KVH, CHUNK, 1024 + 2 * HD), BF16),
        in_specs=[VMEM] * 3,
        out_specs=VMEM,
    )(queries, keys, values)


def pick_kernel(i_ref, *refs):
    copies = [
        pltpu.make_async_copy(
            i_ref.at[pl.ds(4 * n, 4), :, pl.ds(1024, 2 * HD)], refs[n], refs[2].at[n]
        )
        for n in range(2)
    ]
    for copy in copies:
        copy.start()
    for copy in copies:
        copy.wait()


def pick_kv(arrived):
    return pl.pallas_call(
        pick_kernel,
        out_shape=[jax.ShapeDtypeStruct((4, CHUNK, 2 * HD), BF16)] * 2,
        in_specs=[ANY],
        out_specs=[VMEM] * 2,
        scratch_shapes=[pltpu.SemaphoreType.DMA((2,))],
    )(arrived)


def stack_kernel(*refs):
    for n, ref in enumerate(refs[:-1]):
        refs[-1][n] = ref[...]


def stack(blocks):
    return pl.pallas_call(
        stack_kernel,
        out_shape=jax.ShapeDtypeStruct((len(blocks),) + blocks[0].shape, blocks[0].dtype),
        in_specs=[VMEM] * len(blocks),
        out_specs=VMEM,
    )(*blocks)


def join_kernel(i_ref, o_ref):
    for h in range(KVH):
        o_ref[:, h * 1024 : (h + 1) * 1024] = i_ref[h]


def join_heads(pieces):
    return pl.pallas_call(
        join_kernel,
        out_shape=jax.ShapeDtypeStruct((CHUNK, 64 * HD), BF16),
        in_specs=[VMEM],
        out_specs=VMEM,
        compiler_params=SMALL,
    )(pieces)


def split_decay_kernel(own_ref, gain_ref, o_ref):
    row = lax.broadcasted_iota(jnp.int32, (16, 16), 0)
    col = lax.broadcasted_iota(jnp.int32, (16, 16), 1)
    gain = jnp.where(row == col, jnp.broadcast_to(gain_ref[...], (16, 16)), 0.0)
    gain = jnp.broadcast_to(jnp.sum(gain, axis=1, keepdims=True), (16, CHUNK))
    for t in range(16):
        o_ref[t, :, :CHUNK] = own_ref[:, t * CHUNK : (t + 1) * CHUNK]
        o_ref[t, :, CHUNK:] = gain


def split_decay(own, gain):
    return pl.pallas_call(
        split_decay_kernel,
        out_shape=jax.ShapeDtypeStruct((16, 16, 2 * CHUNK), F32),
        in_specs=[VMEM] * 2,
        out_specs=VMEM,
        compiler_params=SMALL,
    )(own, gain)


def attn_kernel(meta_ref, rows_ref, all_ref, *refs):
    own_refs, other_refs, refs = refs[:6], refs[6:12], refs[12:]
    out_ref, m_ref, acc_ref, s_ref, q_ref, kv_ref, vt_ref, o_ref, q_sem, sems, o_sem = refs
    core, y, zl = meta_ref[2, 0], meta_ref[3, 0], meta_ref[3, 1]
    pltpu.make_async_copy(all_ref.at[:, :, pl.ds(0, 1024)], q_ref, q_sem).start()
    for x in range(4):
        for group, of in ((own_refs, core), (other_refs, 1 - core)):
            for dy in range(4):
                for dz in range(2):
                    piece = group[dy].at[dz] if x < 2 else group[4 + dz].at[dy]
                    pltpu.make_async_copy(
                        piece.at[pl.ds(2 * (x % 2), 2)],
                        kv_ref.at[2 * x + of, lax.rem(y + 4 - dy, 4), :, lax.rem(zl + dz, 2)],
                        sems.at[2 * x + of],
                    ).start()

    def arrive(w):
        pltpu.make_async_copy(kv_ref.at[w], kv_ref.at[w], sems.at[w]).wait()

    def prepare(w):
        arrive(w)
        vt_ref[w, :HD, :] = kv_ref[w].reshape(TK, 2 * HD)[:, HD:].T
        vt_ref[w, HD:, :] = jnp.ones((16, TK), BF16)

    def scores(i, j, slot):
        k = kv_ref[j].reshape(TK, 2 * HD)[:, :HD]
        for g in range(NG):
            heads = range(4 * (g % 2), 4 * (g % 2) + 4)
            q = [q_ref[2 * i + g // 2, :, a * HD : (a + 1) * HD] for a in heads]
            s_ref[slot, g] = dot(k, jnp.concatenate(q, axis=0), ((1,), (1,)))

    def absorb(i, j, slot, masked):
        v = vt_ref[j]
        for g in range(NG):
            s = s_ref[slot, g]
            if masked:
                kpos = j * TK + lax.broadcasted_iota(jnp.int32, (TK, RG), 0)
                seen = (kpos <= rows_ref[i, g, 0:1]) & (kpos >= rows_ref[i, g, 1:2])
                s = jnp.where(seen, s, NEG)
            before = m_ref[g]
            top = jnp.maximum(before, jnp.max(s, axis=0, keepdims=True))
            p = jnp.exp2((s - top) * SCORE_EXP2)
            fade = jnp.exp2((before - top) * SCORE_EXP2)
            m_ref[g] = top
            acc_ref[g] = acc_ref[g] * fade + dot(v, p.astype(BF16))

    def reset():
        m_ref[...] = jnp.full_like(m_ref, NEG)
        acc_ref[...] = jnp.zeros_like(acc_ref)

    def window(i):
        return 2 * i + core

    def body(carry):
        i, j, slot = carry
        last = j == window(i)
        i_next = jnp.where(last, i + 1, i)
        i_read = jnp.minimum(i_next, 3)
        j_next = jnp.where(last, meta_ref[0, i_read] // TK, j + 1)
        edge = last | (j * TK < meta_ref[1, i])

        @pl.when(last & (i < 3))
        def _():
            for n in range(2):
                prepare(window(i) + 1 + n)

        @pl.when(edge)
        def _():
            scores(i_read, j_next, 1 - slot)
            absorb(i, j, slot, True)

        @pl.when(jnp.logical_not(edge))
        def _():
            scores(i_read, j_next, 1 - slot)
            absorb(i, j, slot, False)

        @pl.when(last)
        def _():
            for g in range(NG):
                out = (acc_ref[g, :HD] * (1.0 / acc_ref[g, HD : HD + 1])).T.astype(BF16)
                for a in range(4):
                    low = (4 * (g % 2) + a) * HD
                    o_ref[i, g // 2, :, low : low + HD] = out[a * CHUNK : (a + 1) * CHUNK]
            pltpu.make_async_copy(o_ref.at[i], out_ref.at[pl.ds(2 * i, 2)], o_sem.at[i]).start()
            reset()

        return (i_next, j_next, 1 - slot)

    reset()
    prepare(0)

    @pl.when(core == 1)
    def _():
        prepare(1)

    pltpu.make_async_copy(q_ref, q_ref, q_sem).wait()
    start = meta_ref[0, 0] // TK
    scores(0, start, 0)
    lax.while_loop(lambda carry: carry[0] < 4, body, (jnp.int32(0), start, jnp.int32(0)))

    @pl.when(core == 0)
    def _():
        arrive(7)

    for n in range(4):
        pltpu.make_async_copy(o_ref.at[n], out_ref.at[pl.ds(0, 2)], o_sem.at[n]).wait()


def attend(meta, rows, heads, own, other):
    return pl.pallas_call(
        attn_kernel,
        out_shape=jax.ShapeDtypeStruct((8, CHUNK, 1024), BF16),
        in_specs=[SMEM, VMEM] + [ANY] * 13,
        out_specs=ANY,
        scratch_shapes=[
            pltpu.VMEM((NG, 1, RG), F32),
            pltpu.VMEM((NG, HD + 16, RG), F32),
            pltpu.VMEM((2, NG, TK, RG), F32),
            pltpu.VMEM((8, CHUNK, 1024), BF16),
            pltpu.VMEM((8, 4, 2, 2, CHUNK, 2 * HD), BF16),
            pltpu.VMEM((8, HD + 16, TK), BF16),
            pltpu.VMEM((4, 2, CHUNK, 1024), BF16),
            pltpu.SemaphoreType.DMA,
            pltpu.SemaphoreType.DMA((8,)),
            pltpu.SemaphoreType.DMA((4,)),
        ],
        compiler_params=pltpu.CompilerParams(vmem_limit_bytes=60 << 20),
        cost_estimate=pl.CostEstimate(
            flops=12_000_000_000, bytes_accessed=6 << 20, transcendentals=5_000_000
        ),
    )(meta, rows, heads, *own, *other)


def one_minus_exp(u):
    small = -u * (
        1
        + u / 2 * (1 + u / 3 * (1 + u / 4 * (1 + u / 5 * (1 + u / 6 * (1 + u / 7 * (1 + u / 8))))))
    )
    return jnp.where(u > -0.5, small, 1 - jnp.exp(u))


def spread(columns, heads):
    rows = columns.shape[0]
    half = lax.broadcasted_iota(jnp.int32, (rows, 128), 1) // CHUNK
    parts = [
        jnp.take_along_axis(columns, half + h, axis=1, mode="promise_in_bounds")
        for h in range(0, heads, 2)
    ]
    return jnp.concatenate(parts, axis=1)


def running_decay(decay):
    row = lax.broadcasted_iota(jnp.int32, (CHUNK, CHUNK), 0)
    col = lax.broadcasted_iota(jnp.int32, (CHUNK, CHUNK), 1)
    tri = jnp.where(row >= col, 1.0, 0.0).astype(F32)
    return dot(tri, decay, precision=HIGHEST)


def own_columns(ref, place):
    block = ref[:, pl.ds(pl.multiple_of(place // 2 * 128, 128), 128)]
    return jnp.where(place % 2 == 1, block[:, CHUNK:], block[:, :CHUNK])


def state_kernel(place_ref, x_ref, dec_ref, b_ref, s_ref, f_ref, d_ref):
    decay = dec_ref[...].T[:CHUNK]
    run = running_decay(decay)
    drive = jnp.exp(run[CHUNK - 1 :] - run) * jnp.sqrt(one_minus_exp(2.0 * decay))
    end = jnp.exp(run[CHUNK - 1 :])
    high = end.astype(BF16).astype(F32)
    row = lax.broadcasted_iota(jnp.int32, (8, HM), 0)
    parts = jnp.where(row == 0, high, jnp.where(row == 1, end - high, 0.0))
    for k in range(16):
        f_ref[k, :, :16] = drive[:, 16 * k : 16 * k + 16]
        d_ref[k, :, :16] = parts[:, 16 * k : 16 * k + 16]
    b = own_columns(b_ref, place_ref[2])
    b_high = b.astype(BF16)
    b_low = (b - b_high.astype(F32)).astype(BF16)
    b_two = jnp.concatenate([b_high, b_low], axis=0)

    def block(k, carry):
        cols = pl.ds(pl.multiple_of(k * 1024, 1024), 1024)
        z = (x_ref[:, cols].astype(F32) * spread(f_ref[k], 16)).astype(BF16)
        two = dot(b_two, z)
        full = jnp.concatenate([two[:NS] + two[NS:], spread(d_ref[k], 16)], axis=0).astype(BF16)
        for m in range(8):
            s_ref[8 * k + m] = full[:, 128 * m : 128 * (m + 1)]
        return carry

    lax.fori_loop(0, 16, block, 0, unroll=4)


def chunk_states(place, x, dec, b):
    return pl.pallas_call(
        state_kernel,
        out_shape=jax.ShapeDtypeStruct((128, NS + 8, 128), BF16),
        in_specs=[SMEM] + [VMEM] * 3,
        out_specs=VMEM,
        scratch_shapes=[pltpu.VMEM((16, CHUNK, 128), F32), pltpu.VMEM((16, 8, 128), F32)],
        compiler_params=SMALL,
        cost_estimate=pl.CostEstimate(
            flops=2 * 32 * CHUNK * 16384, bytes_accessed=3 << 20, transcendentals=50_000
        ),
    )(place, x, dec, b)


def output_kernel(place_ref, x_ref, dec_ref, b_ref, c_ref, e_ref, y_ref, f_ref, r_ref, g_ref):
    both = dec_ref[...].T
    decay = both[:CHUNK]
    run = running_decay(decay)
    drive = jnp.exp(-run) * jnp.sqrt(one_minus_exp(2.0 * decay))
    reach = jnp.exp(run)
    gain = jnp.broadcast_to(both[CHUNK : CHUNK + 1], (8, HM))
    for k in range(16):
        f_ref[k, :, :16] = drive[:, 16 * k : 16 * k + 16]
        r_ref[k, :, :16] = reach[:, 16 * k : 16 * k + 16]
        g_ref[k, :, :16] = gain[:, 16 * k : 16 * k + 16]
    row = lax.broadcasted_iota(jnp.int32, (CHUNK, CHUNK), 0)
    col = lax.broadcasted_iota(jnp.int32, (CHUNK, CHUNK), 1)
    b = own_columns(b_ref, place_ref[2])
    c = own_columns(c_ref, place_ref[2])
    inner = jnp.where(row >= col, dot(c, b, ((0,), (0,)), HIGHEST), 0.0)
    weights = jnp.concatenate([inner, c.T], axis=1).astype(BF16)

    def block(k, carry):
        cols = pl.ds(pl.multiple_of(k * 1024, 1024), 1024)
        x = x_ref[:, cols].astype(F32)
        z = (x * spread(f_ref[k], 16)).astype(BF16)
        entering = jnp.concatenate([e_ref[8 * k + m] for m in range(8)], axis=1)
        y = dot(weights, jnp.concatenate([z, entering], axis=0))
        y = y * spread(r_ref[k], 16) + spread(g_ref[k], 16)[:1] * x
        y_ref[:, cols] = y.astype(BF16)
        return carry

    lax.fori_loop(0, 16, block, 0, unroll=4)


def chunk_outputs(place, x, dec, b, c, entering):
    return pl.pallas_call(
        output_kernel,
        out_shape=jax.ShapeDtypeStruct((CHUNK, 16384), BF16),
        in_specs=[SMEM] + [VMEM] * 5,
        out_specs=VMEM,
        scratch_shapes=[
            pltpu.VMEM((16, CHUNK, 128), F32),
            pltpu.VMEM((16, CHUNK, 128), F32),
            pltpu.VMEM((16, 8, 128), F32),
        ],
        compiler_params=SMALL,
        cost_estimate=pl.CostEstimate(
            flops=2 * 80 * CHUNK * 16384, bytes_accessed=5 << 20, transcendentals=50_000
        ),
    )(place, x, dec, b, c, entering)


def enter_kernel(s_ref, e_ref):
    def chunk(k, state):
        e_ref[k] = state.astype(BF16)
        arrived = s_ref[k].astype(F32)
        return state * (arrived[NS : NS + 1] + arrived[NS + 1 : NS + 2]) + arrived[:NS]

    lax.fori_loop(0, 128, chunk, jnp.zeros((NS, 128), F32), unroll=8)


def entering_states(states):
    return pl.pallas_call(
        enter_kernel,
        out_shape=jax.ShapeDtypeStruct((128, NS, 128), BF16),
        in_specs=[VMEM],
        out_specs=VMEM,
        compiler_params=SMALL,
        cost_estimate=pl.CostEstimate(
            flops=60_000_000_000, bytes_accessed=2 << 20, transcendentals=0
        ),
    )(states)


def per_device(
    mamba_in, state_in_b, state_out_c, step_decay, skip_gain, queries, keys, values, doc_ids
):
    core, y, zl = lax.axis_index("core"), lax.axis_index("y"), lax.axis_index("zl")
    z = 2 * lax.axis_index("zh") + zl
    spot = jnp.stack([y, z, 4 * y + z]).astype(jnp.int32)
    b, c = state_in_b.T, state_out_c.T

    heads = lax.all_to_all(split_heads(queries, keys, values), HEADS, 0, 0, tiled=True)

    dec, heads = lax.optimization_barrier((split_decay(step_decay.T, skip_gain[None]), heads))
    dec = lax.all_to_all(dec, TP, 0, 0, tiled=True).reshape(HM, 2 * CHUNK)
    def along_z(block):
        return [block, lax.ppermute(block, "zl", [(0, 1), (1, 0)])]

    def along_y(block):
        steps = [[(n, (n + k) % 4) for n in range(4)] for k in range(1, 4)]
        return [block] + [lax.ppermute(block, "y", step) for step in steps]

    lead, tail = pick_kv(heads)
    lead, tail = stack(along_z(lead)), stack(along_y(tail))
    dec, lead, tail = lax.optimization_barrier((dec, lead, tail))
    states = chunk_states(spot, mamba_in, dec, b)
    own = along_y(lead) + along_z(tail)
    other = [lax.ppermute(block, "core", [(0, 1), (1, 0)]) for block in own]
    states = lax.all_to_all(states, ALL, 0, 0, tiled=True)

    blocks = jnp.arange(64, dtype=jnp.int32)
    starts = jnp.sum(doc_ids[None] < doc_ids[:, None], axis=1).astype(jnp.int32) * 128
    row = jnp.arange(1024, dtype=jnp.int32)
    place = (2 * jnp.arange(4)[:, None] + core) * 1024 + row % 64
    place = place + (4 * y + 2 * (row // 512) + zl) * CHUNK
    first = jnp.sum(
        jnp.where(place[:, :, None] // 128 == blocks, starts[None, None], 0), axis=2
    )
    rows = jnp.stack([place, first], axis=1).astype(jnp.int32)
    low, high = jnp.min(first, axis=1), jnp.max(first, axis=1)
    rows = rows.reshape(4, 2, NG, RG).transpose(0, 2, 1, 3)
    ids = jnp.stack([y, zl, y, zl])
    meta = jnp.stack([low, high, jnp.broadcast_to(core, (4,)), ids]).astype(jnp.int32)
    entering = entering_states(states)
    entering, meta = lax.optimization_barrier((entering, meta))
    entering = lax.all_to_all(entering, ALL, 0, 0, tiled=True)
    attn = attend(meta, rows, heads, own, other)
    attn = lax.all_to_all(attn, HEADS, 0, 0, tiled=True)
    mamba_out = chunk_outputs(spot, mamba_in, dec, b, c, entering)
    return (mamba_out, join_heads(attn))


def solution(mesh):
    inner = Mesh(mesh.devices.reshape(4, 2, 4, 2, 2), ALL)
    in_specs = (
        P(ALL, None),
        P(CTX, None),
        P(CTX, None),
        P(CTX, TP),
        P(TP),
        P(ALL, None),
        P(ALL, None),
        P(ALL, None),
        P(),
    )
    out_specs = (P(ALL, None), P(ALL, None))
    return jax.shard_map(
        per_device, mesh=inner, in_specs=in_specs, out_specs=out_specs, check_vma=False
    )
```

```python
import math

import jax
import jax.numpy as jnp
from jax import lax
from jax.experimental import pallas as pl
from jax.experimental.pallas import tpu as pltpu
from jax.sharding import Mesh, PartitionSpec as P

NS = 16
KVH = 8
HD = 128
HM = 256
CHUNK = 64
NEG = -1e30
SCORE_EXP2 = HD**-0.5 * math.log2(math.e)
HIGHEST = lax.Precision.HIGHEST
F32 = jnp.float32
BF16 = jnp.bfloat16
ALL = ("x", "core", "y", "zh", "zl")
CTX = ("x", "core")
TP = ("y", "zh", "zl")
HEADS = ("zl", "x")
VMEM = pl.BlockSpec(memory_space=pltpu.VMEM)
SMEM = pl.BlockSpec(memory_space=pltpu.SMEM)
ANY = pl.BlockSpec(memory_space=pl.ANY)
TK = 1024
NG = 4
RG = 1024 // NG
SMALL = pltpu.CompilerParams(vmem_limit_bytes=16 << 20)


def dot(a, b, dims=((1,), (0,)), precision=None):
    return lax.dot_general(
        a, b, (dims, ((), ())), precision=precision, preferred_element_type=F32
    )


def split_kernel(q_ref, k_ref, v_ref, o_ref):
    for h in range(KVH):
        o_ref[h, :, :1024] = q_ref[:, h * 1024 : (h + 1) * 1024]
        o_ref[h, :, 1024 : 1024 + HD] = k_ref[:, h * HD : (h + 1) * HD]
        o_ref[h, :, 1024 + HD :] = v_ref[:, h * HD : (h + 1) * HD]


def split_heads(queries, keys, values):
    return pl.pallas_call(
        split_kernel,
        out_shape=jax.ShapeDtypeStruct((KVH, CHUNK, 1024 + 2 * HD), BF16),
        in_specs=[VMEM] * 3,
        out_specs=VMEM,
    )(queries, keys, values)


def pick_kernel(i_ref, *refs):
    copies = [
        pltpu.make_async_copy(
            i_ref.at[pl.ds(4 * n, 4), :, pl.ds(1024, 2 * HD)], refs[n], refs[2].at[n]
        )
        for n in range(2)
    ]
    for copy in copies:
        copy.start()
    for copy in copies:
        copy.wait()


def pick_kv(arrived):
    return pl.pallas_call(
        pick_kernel,
        out_shape=[jax.ShapeDtypeStruct((4, CHUNK, 2 * HD), BF16)] * 2,
        in_specs=[ANY],
        out_specs=[VMEM] * 2,
        scratch_shapes=[pltpu.SemaphoreType.DMA((2,))],
    )(arrived)


def stack_kernel(*refs):
    for n, ref in enumerate(refs[:-1]):
        refs[-1][n] = ref[...]


def stack(blocks):
    return pl.pallas_call(
        stack_kernel,
        out_shape=jax.ShapeDtypeStruct((len(blocks),) + blocks[0].shape, blocks[0].dtype),
        in_specs=[VMEM] * len(blocks),
        out_specs=VMEM,
    )(*blocks)


def join_kernel(i_ref, o_ref):
    for h in range(KVH):
        o_ref[:, h * 1024 : (h + 1) * 1024] = i_ref[h]


def join_heads(pieces):
    return pl.pallas_call(
        join_kernel,
        out_shape=jax.ShapeDtypeStruct((CHUNK, 64 * HD), BF16),
        in_specs=[VMEM],
        out_specs=VMEM,
        compiler_params=SMALL,
    )(pieces)


def split_decay_kernel(own_ref, gain_ref, o_ref):
    row = lax.broadcasted_iota(jnp.int32, (16, 16), 0)
    col = lax.broadcasted_iota(jnp.int32, (16, 16), 1)
    gain = jnp.where(row == col, jnp.broadcast_to(gain_ref[...], (16, 16)), 0.0)
    gain = jnp.broadcast_to(jnp.sum(gain, axis=1, keepdims=True), (16, CHUNK))
    for t in range(16):
        o_ref[t, :, :CHUNK] = own_ref[:, t * CHUNK : (t + 1) * CHUNK]
        o_ref[t, :, CHUNK:] = gain


def split_decay(own, gain):
    return pl.pallas_call(
        split_decay_kernel,
        out_shape=jax.ShapeDtypeStruct((16, 16, 2 * CHUNK), F32),
        in_specs=[VMEM] * 2,
        out_specs=VMEM,
        compiler_params=SMALL,
    )(own, gain)


def attn_kernel(meta_ref, all_ref, *refs):
    own_refs, other_refs, refs = refs[:6], refs[6:12], refs[12:]
    out_ref, m_ref, acc_ref, s_ref, q_ref, kv_ref, vt_ref, o_ref, q_sem, sem, o_sem = refs
    core, y, zh = meta_ref[1, 0], meta_ref[1, 1], meta_ref[1, 2]
    for group, of in ((own_refs, core), (other_refs, 1 - core)):
        for dy in range(4):
            for dz in range(2):
                for zl in range(2):
                    piece = group[4 + dz].at[dy] if zl else group[dy].at[dz]
                    place = kv_ref.at[:, of, lax.rem(y + 4 - dy, 4), lax.rem(zh + dz, 2), zl]
                    pltpu.make_async_copy(piece, place, sem).start()
    pltpu.make_async_copy(all_ref.at[:, :, pl.ds(0, 1024)], q_ref, q_sem).start()

    def tile(j):
        return kv_ref[j // 2, j % 2].reshape(TK, 2 * HD)

    def prepare(w):
        vt_ref[w, :HD, :] = tile(w)[:, HD:].T
        vt_ref[w, HD:, :] = jnp.ones((16, TK), BF16)

    def scores(i, j, slot):
        k = tile(j)[:, :HD]
        for g in range(NG):
            heads = range(4 * (g % 2), 4 * (g % 2) + 4)
            q = [q_ref[4 * (g // 2) + i, :, a * HD : (a + 1) * HD] for a in heads]
            s_ref[slot, g] = dot(k, jnp.concatenate(q, axis=0), ((1,), (1,)))

    def absorb(i, j, slot, causal, begins):
        v = vt_ref[j]
        key = lax.broadcasted_iota(jnp.int32, (TK, RG), 0)
        token = lax.broadcasted_iota(jnp.int32, (1, RG), 1) % CHUNK
        at = (2 * i + core - j) * TK + y * 256 + zh * 128 + token
        for g in range(NG):
            s = s_ref[slot, g]
            if causal:
                s = jnp.where(key <= at + CHUNK * (g // 2), s, NEG)
            if begins:
                s = jnp.where(key >= meta_ref[0, i] - j * TK, s, NEG)
            before = m_ref[g]
            top = jnp.maximum(before, jnp.max(s, axis=0, keepdims=True))
            p = jnp.exp2((s - top) * SCORE_EXP2)
            fade = jnp.exp2((before - top) * SCORE_EXP2)
            m_ref[g] = top
            acc_ref[g] = acc_ref[g] * fade + dot(v, p.astype(BF16))

    def reset():
        m_ref[...] = jnp.full_like(m_ref, NEG)
        acc_ref[...] = jnp.zeros_like(acc_ref)

    def body(carry):
        i, j, slot = carry
        last = j == 2 * i + core
        i_next = jnp.where(last, i + 1, i)
        i_read = jnp.minimum(i_next, 3)
        j_next = jnp.where(last, meta_ref[0, i_read] // TK, j + 1)
        begins = j * TK < meta_ref[0, i]
        causal = last & jnp.logical_not(begins)

        @pl.when(last & (i < 3))
        def _():
            for n in range(2):
                prepare(2 * i + core + 1 + n)

        @pl.when(begins)
        def _():
            scores(i_read, j_next, 1 - slot)
            absorb(i, j, slot, True, True)

        @pl.when(causal)
        def _():
            scores(i_read, j_next, 1 - slot)
            absorb(i, j, slot, True, False)

        @pl.when(jnp.logical_not(begins | causal))
        def _():
            scores(i_read, j_next, 1 - slot)
            absorb(i, j, slot, False, False)

        @pl.when(last)
        def _():
            for g in range(NG):
                out = (acc_ref[g, :HD] * (1.0 / acc_ref[g, HD : HD + 1])).T.astype(BF16)
                for a in range(4):
                    low = (4 * (g % 2) + a) * HD
                    o_ref[g // 2, i, :, low : low + HD] = out[a * CHUNK : (a + 1) * CHUNK]
            pltpu.make_async_copy(o_ref.at[:, i], out_ref.at[:, i], o_sem.at[i]).start()
            reset()

        return (i_next, j_next, 1 - slot)

    reset()
    pltpu.make_async_copy(kv_ref, kv_ref, sem).wait()
    prepare(0)

    @pl.when(core == 1)
    def _():
        prepare(1)

    pltpu.make_async_copy(q_ref, q_ref, q_sem).wait()
    start = meta_ref[0, 0] // TK
    scores(0, start, 0)
    lax.while_loop(lambda carry: carry[0] < 4, body, (jnp.int32(0), start, jnp.int32(0)))
    for n in range(4):
        pltpu.make_async_copy(o_ref.at[:, n], out_ref.at[:, n], o_sem.at[n]).wait()


def attend(meta, heads, own, other):
    return pl.pallas_call(
        attn_kernel,
        out_shape=jax.ShapeDtypeStruct((2, 4, CHUNK, 1024), BF16),
        in_specs=[SMEM] + [ANY] * 13,
        out_specs=ANY,
        scratch_shapes=[
            pltpu.VMEM((NG, 1, RG), F32),
            pltpu.VMEM((NG, HD + 16, RG), F32),
            pltpu.VMEM((2, NG, TK, RG), F32),
            pltpu.VMEM((8, CHUNK, 1024), BF16),
            pltpu.VMEM((4, 2, 4, 2, 2, CHUNK, 2 * HD), BF16),
            pltpu.VMEM((8, HD + 16, TK), BF16),
            pltpu.VMEM((2, 4, CHUNK, 1024), BF16),
            pltpu.SemaphoreType.DMA,
            pltpu.SemaphoreType.DMA,
            pltpu.SemaphoreType.DMA((4,)),
        ],
        compiler_params=pltpu.CompilerParams(vmem_limit_bytes=60 << 20),
        cost_estimate=pl.CostEstimate(
            flops=12_000_000_000, bytes_accessed=6 << 20, transcendentals=5_000_000
        ),
    )(meta, heads, *own, *other)


def one_minus_exp(u):
    small = -u * (
        1
        + u / 2 * (1 + u / 3 * (1 + u / 4 * (1 + u / 5 * (1 + u / 6 * (1 + u / 7 * (1 + u / 8))))))
    )
    return jnp.where(u > -0.5, small, 1 - jnp.exp(u))


def spread(columns, heads):
    rows = columns.shape[0]
    half = lax.broadcasted_iota(jnp.int32, (rows, 128), 1) // CHUNK
    parts = [
        jnp.take_along_axis(columns, half + h, axis=1, mode="promise_in_bounds")
        for h in range(0, heads, 2)
    ]
    return jnp.concatenate(parts, axis=1)


def running_decay(decay):
    row = lax.broadcasted_iota(jnp.int32, (CHUNK, CHUNK), 0)
    col = lax.broadcasted_iota(jnp.int32, (CHUNK, CHUNK), 1)
    tri = jnp.where(row >= col, 1.0, 0.0).astype(F32)
    return dot(tri, decay, precision=HIGHEST)


def own_columns(ref, place):
    block = ref[:, pl.ds(pl.multiple_of(place // 2 * 128, 128), 128)]
    return jnp.where(place % 2 == 1, block[:, CHUNK:], block[:, :CHUNK])


def state_kernel(place_ref, x_ref, dec_ref, b_ref, s_ref, f_ref, d_ref):
    decay = dec_ref[...].T[:CHUNK]
    run = running_decay(decay)
    drive = jnp.exp(run[CHUNK - 1 :] - run) * jnp.sqrt(one_minus_exp(2.0 * decay))
    end = jnp.exp(run[CHUNK - 1 :])
    high = end.astype(BF16).astype(F32)
    row = lax.broadcasted_iota(jnp.int32, (8, HM), 0)
    parts = jnp.where(row == 0, high, jnp.where(row == 1, end - high, 0.0))
    for k in range(16):
        f_ref[k, :, :16] = drive[:, 16 * k : 16 * k + 16]
        d_ref[k, :, :16] = parts[:, 16 * k : 16 * k + 16]
    b = own_columns(b_ref, place_ref[2])
    b_high = b.astype(BF16)
    b_low = (b - b_high.astype(F32)).astype(BF16)
    b_two = jnp.concatenate([b_high, b_low], axis=0)

    def block(k, carry):
        cols = pl.ds(pl.multiple_of(k * 1024, 1024), 1024)
        z = (x_ref[:, cols].astype(F32) * spread(f_ref[k], 16)).astype(BF16)
        two = dot(b_two, z)
        full = jnp.concatenate([two[:NS] + two[NS:], spread(d_ref[k], 16)], axis=0).astype(BF16)
        for m in range(8):
            s_ref[8 * k + m] = full[:, 128 * m : 128 * (m + 1)]
        return carry

    lax.fori_loop(0, 16, block, 0, unroll=4)


def chunk_states(place, x, dec, b):
    return pl.pallas_call(
        state_kernel,
        out_shape=jax.ShapeDtypeStruct((128, NS + 8, 128), BF16),
        in_specs=[SMEM] + [VMEM] * 3,
        out_specs=VMEM,
        scratch_shapes=[pltpu.VMEM((16, CHUNK, 128), F32), pltpu.VMEM((16, 8, 128), F32)],
        compiler_params=SMALL,
        cost_estimate=pl.CostEstimate(
            flops=30_000_000_000, bytes_accessed=3 << 20, transcendentals=50_000
        ),
    )(place, x, dec, b)


def output_kernel(place_ref, x_ref, dec_ref, b_ref, c_ref, e_ref, y_ref, f_ref, r_ref, g_ref):
    both = dec_ref[...].T
    decay = both[:CHUNK]
    run = running_decay(decay)
    drive = jnp.exp(-run) * jnp.sqrt(one_minus_exp(2.0 * decay))
    reach = jnp.exp(run)
    gain = jnp.broadcast_to(both[CHUNK : CHUNK + 1], (8, HM))
    for k in range(16):
        f_ref[k, :, :16] = drive[:, 16 * k : 16 * k + 16]
        r_ref[k, :, :16] = reach[:, 16 * k : 16 * k + 16]
        g_ref[k, :, :16] = gain[:, 16 * k : 16 * k + 16]
    row = lax.broadcasted_iota(jnp.int32, (CHUNK, CHUNK), 0)
    col = lax.broadcasted_iota(jnp.int32, (CHUNK, CHUNK), 1)
    b = own_columns(b_ref, place_ref[2])
    c = own_columns(c_ref, place_ref[2])
    inner = jnp.where(row >= col, dot(c, b, ((0,), (0,)), HIGHEST), 0.0)
    weights = jnp.concatenate([inner, c.T], axis=1).astype(BF16)

    def block(k, carry):
        cols = pl.ds(pl.multiple_of(k * 1024, 1024), 1024)
        x = x_ref[:, cols].astype(F32)
        z = (x * spread(f_ref[k], 16)).astype(BF16)
        entering = jnp.concatenate([e_ref[8 * k + m] for m in range(8)], axis=1)
        y = dot(weights, jnp.concatenate([z, entering], axis=0))
        y = y * spread(r_ref[k], 16) + spread(g_ref[k], 16)[:1] * x
        y_ref[:, cols] = y.astype(BF16)
        return carry

    lax.fori_loop(0, 16, block, 0, unroll=4)


def chunk_outputs(place, x, dec, b, c, entering):
    return pl.pallas_call(
        output_kernel,
        out_shape=jax.ShapeDtypeStruct((CHUNK, 16384), BF16),
        in_specs=[SMEM] + [VMEM] * 5,
        out_specs=VMEM,
        scratch_shapes=[
            pltpu.VMEM((16, CHUNK, 128), F32),
            pltpu.VMEM((16, CHUNK, 128), F32),
            pltpu.VMEM((16, 8, 128), F32),
        ],
        compiler_params=SMALL,
        cost_estimate=pl.CostEstimate(
            flops=2 * 80 * CHUNK * 16384, bytes_accessed=5 << 20, transcendentals=50_000
        ),
    )(place, x, dec, b, c, entering)


def enter_kernel(s_ref, e_ref):
    def chunk(k, state):
        e_ref[k] = state.astype(BF16)
        arrived = s_ref[k].astype(F32)
        return state * (arrived[NS : NS + 1] + arrived[NS + 1 : NS + 2]) + arrived[:NS]

    lax.fori_loop(0, 128, chunk, jnp.zeros((NS, 128), F32), unroll=8)


def entering_states(states):
    return pl.pallas_call(
        enter_kernel,
        out_shape=jax.ShapeDtypeStruct((128, NS, 128), BF16),
        in_specs=[VMEM],
        out_specs=VMEM,
        compiler_params=SMALL,
        cost_estimate=pl.CostEstimate(
            flops=60_000_000_000, bytes_accessed=2 << 20, transcendentals=0
        ),
    )(states)


def per_device(
    mamba_in, state_in_b, state_out_c, step_decay, skip_gain, queries, keys, values, doc_ids
):
    core, y, zh = lax.axis_index("core"), lax.axis_index("y"), lax.axis_index("zh")
    z = 2 * zh + lax.axis_index("zl")
    spot = jnp.stack([y, z, 4 * y + z]).astype(jnp.int32)
    b, c = state_in_b.T, state_out_c.T

    heads = lax.all_to_all(split_heads(queries, keys, values), HEADS, 0, 0, tiled=True)

    dec, heads = lax.optimization_barrier((split_decay(step_decay.T, skip_gain[None]), heads))
    dec = lax.all_to_all(dec, TP, 0, 0, tiled=True).reshape(HM, 2 * CHUNK)
    def along_z(block):
        return [block, lax.ppermute(block, "zh", [(0, 1), (1, 0)])]

    def along_y(block):
        steps = [[(n, (n + k) % 4) for n in range(4)] for k in range(1, 4)]
        return [block] + [lax.ppermute(block, "y", step) for step in steps]

    lead, tail = pick_kv(heads)
    lead, tail = stack(along_z(lead)), stack(along_y(tail))
    states = chunk_states(spot, mamba_in, dec, b)
    states, lead, tail = lax.optimization_barrier((states, lead, tail))
    own = along_y(lead) + along_z(tail)
    other = [lax.ppermute(block, "core", [(0, 1), (1, 0)]) for block in own]
    states = lax.all_to_all(states, ALL, 0, 0, tiled=True)

    blocks = jnp.arange(64)
    mine = (2 * jnp.arange(4)[:, None] + core) * 8 + 2 * y + zh
    doc = jnp.sum(jnp.where(blocks[None] == mine, doc_ids[None], 0), axis=1)
    first = jnp.sum(doc_ids[None] < doc[:, None], axis=1) * 128
    meta = jnp.stack([first, jnp.stack([core, y, zh, zh])]).astype(jnp.int32)
    entering = entering_states(states)
    entering, meta = lax.optimization_barrier((entering, meta))
    entering = lax.all_to_all(entering, ALL, 0, 0, tiled=True)
    attn = attend(meta, heads, own, other).reshape(8, CHUNK, 1024)
    attn = lax.all_to_all(attn, HEADS, 0, 0, tiled=True)
    mamba_out = chunk_outputs(spot, mamba_in, dec, b, c, entering)
    return (mamba_out, join_heads(attn))


def solution(mesh):
    inner = Mesh(mesh.devices.reshape(4, 2, 4, 2, 2), ALL)
    in_specs = (
        P(ALL, None),
        P(CTX, None),
        P(CTX, None),
        P(CTX, TP),
        P(TP),
        P(ALL, None),
        P(ALL, None),
        P(ALL, None),
        P(),
    )
    out_specs = (P(ALL, None), P(ALL, None))
    return jax.shard_map(
        per_device, mesh=inner, in_specs=in_specs, out_specs=out_specs, check_vma=False
    )
```

```python
import math

import jax
import jax.numpy as jnp
from jax import lax
from jax.experimental import pallas as pl
from jax.experimental.pallas import tpu as pltpu
from jax.sharding import Mesh, PartitionSpec as P

NS = 16
KVH = 8
HD = 128
HM = 256
CHUNK = 64
NEG = -1e30
SCORE_EXP2 = HD**-0.5 * math.log2(math.e)
HIGHEST = lax.Precision.HIGHEST
F32 = jnp.float32
BF16 = jnp.bfloat16
ALL = ("x", "core", "y", "zh", "zl")
CTX = ("x", "core")
TP = ("y", "zh", "zl")
HEADS = ("zl", "x")
VMEM = pl.BlockSpec(memory_space=pltpu.VMEM)
SMEM = pl.BlockSpec(memory_space=pltpu.SMEM)
ANY = pl.BlockSpec(memory_space=pl.ANY)
TK = 1024
NG = 4
RG = 1024 // NG
SMALL = pltpu.CompilerParams(vmem_limit_bytes=16 << 20)


def dot(a, b, dims=((1,), (0,)), precision=None):
    return lax.dot_general(
        a, b, (dims, ((), ())), precision=precision, preferred_element_type=F32
    )


def split_kernel(q_ref, k_ref, v_ref, o_ref):
    for h in range(KVH):
        o_ref[h, :, :1024] = q_ref[:, h * 1024 : (h + 1) * 1024]
        o_ref[h, :, 1024 : 1024 + HD] = k_ref[:, h * HD : (h + 1) * HD]
        o_ref[h, :, 1024 + HD :] = v_ref[:, h * HD : (h + 1) * HD]


def split_heads(queries, keys, values):
    return pl.pallas_call(
        split_kernel,
        out_shape=jax.ShapeDtypeStruct((KVH, CHUNK, 1024 + 2 * HD), BF16),
        in_specs=[VMEM] * 3,
        out_specs=VMEM,
    )(queries, keys, values)


def pick_kernel(i_ref, *refs):
    copies = [
        pltpu.make_async_copy(
            i_ref.at[pl.ds(4 * n, 4), :, pl.ds(1024, 2 * HD)], refs[n], refs[2].at[n]
        )
        for n in range(2)
    ]
    for copy in copies:
        copy.start()
    for copy in copies:
        copy.wait()


def pick_kv(arrived):
    return pl.pallas_call(
        pick_kernel,
        out_shape=[jax.ShapeDtypeStruct((4, CHUNK, 2 * HD), BF16)] * 2,
        in_specs=[ANY],
        out_specs=[VMEM] * 2,
        scratch_shapes=[pltpu.SemaphoreType.DMA((2,))],
    )(arrived)


def stack_kernel(*refs):
    for n, ref in enumerate(refs[:-1]):
        refs[-1][n] = ref[...]


def stack(blocks):
    return pl.pallas_call(
        stack_kernel,
        out_shape=jax.ShapeDtypeStruct((len(blocks),) + blocks[0].shape, blocks[0].dtype),
        in_specs=[VMEM] * len(blocks),
        out_specs=VMEM,
    )(*blocks)


def join_kernel(i_ref, o_ref):
    for h in range(KVH):
        o_ref[:, h * 1024 : (h + 1) * 1024] = i_ref[h]


def join_heads(pieces):
    return pl.pallas_call(
        join_kernel,
        out_shape=jax.ShapeDtypeStruct((CHUNK, 64 * HD), BF16),
        in_specs=[VMEM],
        out_specs=VMEM,
        compiler_params=SMALL,
    )(pieces)


def split_decay_kernel(own_ref, gain_ref, o_ref):
    row = lax.broadcasted_iota(jnp.int32, (16, 16), 0)
    col = lax.broadcasted_iota(jnp.int32, (16, 16), 1)
    gain = jnp.where(row == col, jnp.broadcast_to(gain_ref[...], (16, 16)), 0.0)
    gain = jnp.broadcast_to(jnp.sum(gain, axis=1, keepdims=True), (16, CHUNK))
    for t in range(16):
        o_ref[t, :, :CHUNK] = own_ref[:, t * CHUNK : (t + 1) * CHUNK]
        o_ref[t, :, CHUNK:] = gain


def split_decay(own, gain):
    return pl.pallas_call(
        split_decay_kernel,
        out_shape=jax.ShapeDtypeStruct((16, 16, 2 * CHUNK), F32),
        in_specs=[VMEM] * 2,
        out_specs=VMEM,
        compiler_params=SMALL,
    )(own, gain)


def attn_kernel(meta_ref, all_ref, *refs):
    own_refs, other_refs, refs = refs[:6], refs[6:12], refs[12:]
    out_ref, m_ref, acc_ref, *s_refs, q_ref, kv_ref, vt_ref, o_ref, q_sem, sem, o_sem = refs
    core, y, zh = meta_ref[1, 0], meta_ref[1, 1], meta_ref[1, 2]
    for group, of in ((own_refs, core), (other_refs, 1 - core)):
        for dy in range(4):
            for dz in range(2):
                for zl in range(2):
                    piece = group[4 + dz].at[dy] if zl else group[dy].at[dz]
                    place = kv_ref.at[:, of, lax.rem(y + 4 - dy, 4), lax.rem(zh + dz, 2), zl]
                    pltpu.make_async_copy(piece, place, sem).start()
    pltpu.make_async_copy(all_ref.at[:, :, pl.ds(0, 1024)], q_ref, q_sem).start()

    def tile(j):
        return kv_ref[j // 2, j % 2].reshape(TK, 2 * HD)

    def prepare(w):
        vt_ref[w, :HD, :] = tile(w)[:, HD:].T
        vt_ref[w, HD:, :] = jnp.ones((16, TK), BF16)

    def scores(i, j, slot, groups):
        k = tile(j)[:, :HD]
        for g in groups:
            heads = range(4 * (g % 2), 4 * (g % 2) + 4)
            q = [q_ref[4 * (g // 2) + i, :, a * HD : (a + 1) * HD] for a in heads]
            s_refs[slot][g] = dot(k, jnp.concatenate(q, axis=0), ((1,), (1,)))

    def absorb(i, j, slot, causal, begins, groups):
        v = vt_ref[j]
        key = lax.broadcasted_iota(jnp.int32, (TK, RG), 0)
        token = lax.broadcasted_iota(jnp.int32, (1, RG), 1) % CHUNK
        at = (2 * i + core - j) * TK + y * 256 + zh * 128 + token
        for g in groups:
            s = s_refs[slot][g]
            if causal:
                s = jnp.where(key <= at + CHUNK * (g // 2), s, NEG)
            if begins:
                s = jnp.where(key >= meta_ref[0, i] - j * TK, s, NEG)
            before = m_ref[g]
            top = jnp.maximum(before, jnp.max(s, axis=0, keepdims=True))
            p = jnp.exp2((s - top) * SCORE_EXP2)
            fade = jnp.exp2((before - top) * SCORE_EXP2)
            m_ref[g] = top
            acc_ref[g] = acc_ref[g] * fade + dot(v, p.astype(BF16))

    def step(i_read, j_next, i, j, now, causal, begins):
        for g in range(NG):
            scores(i_read, j_next, 1 - now, [g])
            absorb(i, j, now, causal, begins, [g])

    def reset():
        m_ref[...] = jnp.full_like(m_ref, NEG)
        acc_ref[...] = jnp.zeros_like(acc_ref)

    def body(carry):
        i, j, slot = carry
        last = j == 2 * i + core
        i_next = jnp.where(last, i + 1, i)
        i_read = jnp.minimum(i_next, 3)
        j_next = jnp.where(last, meta_ref[0, i_read] // TK, j + 1)
        begins = j * TK < meta_ref[0, i]
        causal = last & jnp.logical_not(begins)

        @pl.when(last & (i < 3))
        def _():
            for n in range(2):
                prepare(2 * i + core + 1 + n)

        for now in range(2):
            turn = slot == now

            @pl.when(turn & begins)
            def _(now=now):
                step(i_read, j_next, i, j, now, True, True)

            @pl.when(turn & causal)
            def _(now=now):
                step(i_read, j_next, i, j, now, True, False)

            @pl.when(turn & jnp.logical_not(begins | causal))
            def _(now=now):
                step(i_read, j_next, i, j, now, False, False)

        @pl.when(last)
        def _():
            for g in range(NG):
                out = (acc_ref[g, :HD] * (1.0 / acc_ref[g, HD : HD + 1])).T.astype(BF16)
                for a in range(4):
                    low = (4 * (g % 2) + a) * HD
                    o_ref[g // 2, i, :, low : low + HD] = out[a * CHUNK : (a + 1) * CHUNK]
            pltpu.make_async_copy(o_ref.at[:, i], out_ref.at[:, i], o_sem.at[i]).start()
            reset()

        return (i_next, j_next, 1 - slot)

    reset()
    pltpu.make_async_copy(kv_ref, kv_ref, sem).wait()
    prepare(0)

    @pl.when(core == 1)
    def _():
        prepare(1)

    pltpu.make_async_copy(q_ref, q_ref, q_sem).wait()
    start = meta_ref[0, 0] // TK
    scores(0, start, 0, range(NG))
    lax.while_loop(lambda carry: carry[0] < 4, body, (jnp.int32(0), start, jnp.int32(0)))
    for n in range(4):
        pltpu.make_async_copy(o_ref.at[:, n], out_ref.at[:, n], o_sem.at[n]).wait()


def attend(meta, heads, own, other):
    return pl.pallas_call(
        attn_kernel,
        out_shape=jax.ShapeDtypeStruct((2, 4, CHUNK, 1024), BF16),
        in_specs=[SMEM] + [ANY] * 13,
        out_specs=ANY,
        scratch_shapes=[
            pltpu.VMEM((NG, 1, RG), F32),
            pltpu.VMEM((NG, HD + 16, RG), F32),
            pltpu.VMEM((NG, TK, RG), F32),
            pltpu.VMEM((NG, TK, RG), F32),
            pltpu.VMEM((8, CHUNK, 1024), BF16),
            pltpu.VMEM((4, 2, 4, 2, 2, CHUNK, 2 * HD), BF16),
            pltpu.VMEM((8, HD + 16, TK), BF16),
            pltpu.VMEM((2, 4, CHUNK, 1024), BF16),
            pltpu.SemaphoreType.DMA,
            pltpu.SemaphoreType.DMA,
            pltpu.SemaphoreType.DMA((4,)),
        ],
        compiler_params=pltpu.CompilerParams(vmem_limit_bytes=60 << 20),
        cost_estimate=pl.CostEstimate(
            flops=12_000_000_000, bytes_accessed=6 << 20, transcendentals=5_000_000
        ),
    )(meta, heads, *own, *other)


def one_minus_exp(u):
    small = -u * (
        1
        + u / 2 * (1 + u / 3 * (1 + u / 4 * (1 + u / 5 * (1 + u / 6 * (1 + u / 7 * (1 + u / 8))))))
    )
    return jnp.where(u > -0.5, small, 1 - jnp.exp(u))


def spread(columns, heads):
    rows = columns.shape[0]
    half = lax.broadcasted_iota(jnp.int32, (rows, 128), 1) // CHUNK
    parts = [
        jnp.take_along_axis(columns, half + h, axis=1, mode="promise_in_bounds")
        for h in range(0, heads, 2)
    ]
    return jnp.concatenate(parts, axis=1)


def running_decay(decay):
    row = lax.broadcasted_iota(jnp.int32, (CHUNK, CHUNK), 0)
    col = lax.broadcasted_iota(jnp.int32, (CHUNK, CHUNK), 1)
    tri = jnp.where(row >= col, 1.0, 0.0).astype(F32)
    return dot(tri, decay, precision=HIGHEST)


def own_columns(ref, place):
    block = ref[:, pl.ds(pl.multiple_of(place // 2 * 128, 128), 128)]
    return jnp.where(place % 2 == 1, block[:, CHUNK:], block[:, :CHUNK])


def state_kernel(place_ref, x_ref, dec_ref, b_ref, s_ref, f_ref, d_ref):
    decay = dec_ref[...].T[:CHUNK]
    run = running_decay(decay)
    drive = jnp.exp(run[CHUNK - 1 :] - run) * jnp.sqrt(one_minus_exp(2.0 * decay))
    end = jnp.exp(run[CHUNK - 1 :])
    high = end.astype(BF16).astype(F32)
    row = lax.broadcasted_iota(jnp.int32, (8, HM), 0)
    parts = jnp.where(row == 0, high, jnp.where(row == 1, end - high, 0.0))
    for k in range(16):
        f_ref[k, :, :16] = drive[:, 16 * k : 16 * k + 16]
        d_ref[k, :, :16] = parts[:, 16 * k : 16 * k + 16]
    b = own_columns(b_ref, place_ref[2])
    b_high = b.astype(BF16)
    b_low = (b - b_high.astype(F32)).astype(BF16)
    b_two = jnp.concatenate([b_high, b_low], axis=0)

    def block(k, carry):
        cols = pl.ds(pl.multiple_of(k * 1024, 1024), 1024)
        z = (x_ref[:, cols].astype(F32) * spread(f_ref[k], 16)).astype(BF16)
        two = dot(b_two, z)
        full = jnp.concatenate([two[:NS] + two[NS:], spread(d_ref[k], 16)], axis=0).astype(BF16)
        for m in range(8):
            s_ref[8 * k + m] = full[:, 128 * m : 128 * (m + 1)]
        return carry

    lax.fori_loop(0, 16, block, 0, unroll=4)


def chunk_states(place, x, dec, b):
    return pl.pallas_call(
        state_kernel,
        out_shape=jax.ShapeDtypeStruct((128, NS + 8, 128), BF16),
        in_specs=[SMEM] + [VMEM] * 3,
        out_specs=VMEM,
        scratch_shapes=[pltpu.VMEM((16, CHUNK, 128), F32), pltpu.VMEM((16, 8, 128), F32)],
        compiler_params=SMALL,
        cost_estimate=pl.CostEstimate(
            flops=30_000_000_000, bytes_accessed=3 << 20, transcendentals=50_000
        ),
    )(place, x, dec, b)


def output_kernel(place_ref, x_ref, dec_ref, b_ref, c_ref, e_ref, y_ref, f_ref, r_ref, g_ref):
    both = dec_ref[...].T
    decay = both[:CHUNK]
    run = running_decay(decay)
    drive = jnp.exp(-run) * jnp.sqrt(one_minus_exp(2.0 * decay))
    reach = jnp.exp(run)
    gain = jnp.broadcast_to(both[CHUNK : CHUNK + 1], (8, HM))
    for k in range(16):
        f_ref[k, :, :16] = drive[:, 16 * k : 16 * k + 16]
        r_ref[k, :, :16] = reach[:, 16 * k : 16 * k + 16]
        g_ref[k, :, :16] = gain[:, 16 * k : 16 * k + 16]
    row = lax.broadcasted_iota(jnp.int32, (CHUNK, CHUNK), 0)
    col = lax.broadcasted_iota(jnp.int32, (CHUNK, CHUNK), 1)
    b = own_columns(b_ref, place_ref[2])
    c = own_columns(c_ref, place_ref[2])
    inner = jnp.where(row >= col, dot(c, b, ((0,), (0,)), HIGHEST), 0.0)
    weights = jnp.concatenate([inner, c.T], axis=1).astype(BF16)

    def block(k, carry):
        cols = pl.ds(pl.multiple_of(k * 1024, 1024), 1024)
        x = x_ref[:, cols].astype(F32)
        z = (x * spread(f_ref[k], 16)).astype(BF16)
        entering = jnp.concatenate([e_ref[8 * k + m] for m in range(8)], axis=1)
        y = dot(weights, jnp.concatenate([z, entering], axis=0))
        y = y * spread(r_ref[k], 16) + spread(g_ref[k], 16)[:1] * x
        y_ref[:, cols] = y.astype(BF16)
        return carry

    lax.fori_loop(0, 16, block, 0, unroll=4)


def chunk_outputs(place, x, dec, b, c, entering):
    return pl.pallas_call(
        output_kernel,
        out_shape=jax.ShapeDtypeStruct((CHUNK, 16384), BF16),
        in_specs=[SMEM] + [VMEM] * 5,
        out_specs=VMEM,
        scratch_shapes=[
            pltpu.VMEM((16, CHUNK, 128), F32),
            pltpu.VMEM((16, CHUNK, 128), F32),
            pltpu.VMEM((16, 8, 128), F32),
        ],
        compiler_params=SMALL,
        cost_estimate=pl.CostEstimate(
            flops=2 * 80 * CHUNK * 16384, bytes_accessed=5 << 20, transcendentals=50_000
        ),
    )(place, x, dec, b, c, entering)


def enter_kernel(s_ref, e_ref):
    def chunk(k, state):
        e_ref[k] = state.astype(BF16)
        arrived = s_ref[k].astype(F32)
        return state * (arrived[NS : NS + 1] + arrived[NS + 1 : NS + 2]) + arrived[:NS]

    lax.fori_loop(0, 128, chunk, jnp.zeros((NS, 128), F32), unroll=8)


def entering_states(states):
    return pl.pallas_call(
        enter_kernel,
        out_shape=jax.ShapeDtypeStruct((128, NS, 128), BF16),
        in_specs=[VMEM],
        out_specs=VMEM,
        compiler_params=SMALL,
        cost_estimate=pl.CostEstimate(
            flops=60_000_000_000, bytes_accessed=2 << 20, transcendentals=0
        ),
    )(states)


def per_device(
    mamba_in, state_in_b, state_out_c, step_decay, skip_gain, queries, keys, values, doc_ids
):
    core, y, zh = lax.axis_index("core"), lax.axis_index("y"), lax.axis_index("zh")
    z = 2 * zh + lax.axis_index("zl")
    spot = jnp.stack([y, z, 4 * y + z]).astype(jnp.int32)
    b, c = state_in_b.T, state_out_c.T

    heads = lax.all_to_all(split_heads(queries, keys, values), HEADS, 0, 0, tiled=True)

    dec, heads = lax.optimization_barrier((split_decay(step_decay.T, skip_gain[None]), heads))
    dec = lax.all_to_all(dec, TP, 0, 0, tiled=True).reshape(HM, 2 * CHUNK)
    def along_z(block):
        return [block, lax.ppermute(block, "zh", [(0, 1), (1, 0)])]

    def along_y(block):
        steps = [[(n, (n + k) % 4) for n in range(4)] for k in range(1, 4)]
        return [block] + [lax.ppermute(block, "y", step) for step in steps]

    lead, tail = pick_kv(heads)
    lead, tail = stack(along_z(lead)), stack(along_y(tail))
    states = chunk_states(spot, mamba_in, dec, b)
    states, lead, tail = lax.optimization_barrier((states, lead, tail))
    own = along_y(lead) + along_z(tail)
    other = [lax.ppermute(block, "core", [(0, 1), (1, 0)]) for block in own]
    states = lax.all_to_all(states, ALL, 0, 0, tiled=True)

    blocks = jnp.arange(64)
    mine = (2 * jnp.arange(4)[:, None] + core) * 8 + 2 * y + zh
    doc = jnp.sum(jnp.where(blocks[None] == mine, doc_ids[None], 0), axis=1)
    first = jnp.sum(doc_ids[None] < doc[:, None], axis=1) * 128
    meta = jnp.stack([first, jnp.stack([core, y, zh, zh])]).astype(jnp.int32)
    entering = entering_states(states)
    entering, meta = lax.optimization_barrier((entering, meta))
    entering = lax.all_to_all(entering, ALL, 0, 0, tiled=True)
    attn = attend(meta, heads, own, other).reshape(8, CHUNK, 1024)
    attn = lax.all_to_all(attn, HEADS, 0, 0, tiled=True)
    mamba_out = chunk_outputs(spot, mamba_in, dec, b, c, entering)
    return (mamba_out, join_heads(attn))


def solution(mesh):
    inner = Mesh(mesh.devices.reshape(4, 2, 4, 2, 2), ALL)
    in_specs = (
        P(ALL, None),
        P(CTX, None),
        P(CTX, None),
        P(CTX, TP),
        P(TP),
        P(ALL, None),
        P(ALL, None),
        P(ALL, None),
        P(),
    )
    out_specs = (P(ALL, None), P(ALL, None))
    return jax.shard_map(
        per_device, mesh=inner, in_specs=in_specs, out_specs=out_specs, check_vma=False
    )
```

```python
import math

import jax
import jax.numpy as jnp
from jax import lax
from jax.experimental import pallas as pl
from jax.experimental.pallas import tpu as pltpu
from jax.sharding import Mesh, PartitionSpec as P

NS = 16
KVH = 8
HD = 128
HM = 256
CHUNK = 64
NEG = -1e30
SCORE_EXP2 = HD**-0.5 * math.log2(math.e)
HIGHEST = lax.Precision.HIGHEST
F32 = jnp.float32
BF16 = jnp.bfloat16
ALL = ("x", "core", "y", "zh", "zl")
CTX = ("x", "core")
TP = ("y", "zh", "zl")
HEADS = ("zl", "x")
VMEM = pl.BlockSpec(memory_space=pltpu.VMEM)
SMEM = pl.BlockSpec(memory_space=pltpu.SMEM)
ANY = pl.BlockSpec(memory_space=pl.ANY)
TK = 1024
NG = 4
RG = 1024 // NG
SMALL = pltpu.CompilerParams(vmem_limit_bytes=16 << 20)


def dot(a, b, dims=((1,), (0,)), precision=None):
    return lax.dot_general(
        a, b, (dims, ((), ())), precision=precision, preferred_element_type=F32
    )


def split_kernel(q_ref, k_ref, v_ref, o_ref):
    for h in range(KVH):
        o_ref[h, :, :1024] = q_ref[:, h * 1024 : (h + 1) * 1024]
        o_ref[h, :, 1024 : 1024 + HD] = k_ref[:, h * HD : (h + 1) * HD]
        o_ref[h, :, 1024 + HD :] = v_ref[:, h * HD : (h + 1) * HD]


def split_heads(queries, keys, values):
    return pl.pallas_call(
        split_kernel,
        out_shape=jax.ShapeDtypeStruct((KVH, CHUNK, 1024 + 2 * HD), BF16),
        in_specs=[VMEM] * 3,
        out_specs=VMEM,
    )(queries, keys, values)


def pick_kernel(i_ref, *refs):
    copies = [
        pltpu.make_async_copy(
            i_ref.at[pl.ds(4 * n, 4), :, pl.ds(1024, 2 * HD)], refs[n], refs[2].at[n]
        )
        for n in range(2)
    ]
    for copy in copies:
        copy.start()
    for copy in copies:
        copy.wait()


def pick_kv(arrived):
    return pl.pallas_call(
        pick_kernel,
        out_shape=[jax.ShapeDtypeStruct((4, CHUNK, 2 * HD), BF16)] * 2,
        in_specs=[ANY],
        out_specs=[VMEM] * 2,
        scratch_shapes=[pltpu.SemaphoreType.DMA((2,))],
    )(arrived)


def stack_kernel(*refs):
    for n, ref in enumerate(refs[:-1]):
        refs[-1][n] = ref[...]


def stack(blocks):
    return pl.pallas_call(
        stack_kernel,
        out_shape=jax.ShapeDtypeStruct((len(blocks),) + blocks[0].shape, blocks[0].dtype),
        in_specs=[VMEM] * len(blocks),
        out_specs=VMEM,
        compiler_params=SMALL,
    )(*blocks)


def join_kernel(i_ref, o_ref):
    for h in range(KVH):
        o_ref[:, h * 1024 : (h + 1) * 1024] = i_ref[h]


def join_heads(pieces):
    return pl.pallas_call(
        join_kernel,
        out_shape=jax.ShapeDtypeStruct((CHUNK, 64 * HD), BF16),
        in_specs=[VMEM],
        out_specs=VMEM,
        compiler_params=SMALL,
    )(pieces)


def split_decay_kernel(own_ref, gain_ref, o_ref):
    row = lax.broadcasted_iota(jnp.int32, (16, 16), 0)
    col = lax.broadcasted_iota(jnp.int32, (16, 16), 1)
    gain = jnp.where(row == col, jnp.broadcast_to(gain_ref[...], (16, 16)), 0.0)
    gain = jnp.broadcast_to(jnp.sum(gain, axis=1, keepdims=True), (16, CHUNK))
    for t in range(16):
        o_ref[t, :, :CHUNK] = own_ref[:, t * CHUNK : (t + 1) * CHUNK]
        o_ref[t, :, CHUNK:] = gain


def split_decay(own, gain):
    return pl.pallas_call(
        split_decay_kernel,
        out_shape=jax.ShapeDtypeStruct((16, 16, 2 * CHUNK), F32),
        in_specs=[VMEM] * 2,
        out_specs=VMEM,
        compiler_params=SMALL,
    )(own, gain)


def attn_kernel(meta_ref, all_ref, *refs):
    own_refs, other_refs, refs = refs[:6], refs[6:12], refs[12:]
    out_ref, m_ref, acc_ref, *s_refs, q_ref, kv_ref, vt_ref, o_ref, q_sem, sem, o_sem = refs
    core, y, zh = meta_ref[1, 0], meta_ref[1, 1], meta_ref[1, 2]
    for group, of in ((own_refs, core), (other_refs, 1 - core)):
        for dy in range(4):
            for dz in range(2):
                for zl in range(2):
                    piece = group[4 + dz].at[dy] if zl else group[dy].at[dz]
                    place = kv_ref.at[:, of, lax.rem(y + 4 - dy, 4), lax.rem(zh + dz, 2), zl]
                    pltpu.make_async_copy(piece, place, sem).start()
    pltpu.make_async_copy(all_ref.at[:, :, pl.ds(0, 1024)], q_ref, q_sem).start()

    def tile(j):
        return kv_ref[j // 2, j % 2].reshape(TK, 2 * HD)

    def prepare(w):
        vt_ref[w, :HD, :] = tile(w)[:, HD:].T
        vt_ref[w, HD:, :] = jnp.ones((16, TK), BF16)

    def scores(i, j, slot, groups):
        k = tile(j)[:, :HD]
        for g in groups:
            heads = range(4 * (g % 2), 4 * (g % 2) + 4)
            q = [q_ref[4 * (g // 2) + i, :, a * HD : (a + 1) * HD] for a in heads]
            s_refs[slot][g] = dot(k, jnp.concatenate(q, axis=0), ((1,), (1,)))

    def absorb(i, j, slot, causal, begins, groups):
        v = vt_ref[j]
        key = lax.broadcasted_iota(jnp.int32, (TK, RG), 0)
        token = lax.broadcasted_iota(jnp.int32, (1, RG), 1) % CHUNK
        at = (2 * i + core - j) * TK + y * 256 + zh * 128 + token
        for g in groups:
            s = s_refs[slot][g]
            if causal:
                s = jnp.where(key <= at + CHUNK * (g // 2), s, NEG)
            if begins:
                s = jnp.where(key >= meta_ref[0, i] - j * TK, s, NEG)
            before = m_ref[g]
            top = jnp.maximum(before, jnp.max(s, axis=0, keepdims=True))
            p = jnp.exp2((s - top) * SCORE_EXP2)
            fade = jnp.exp2((before - top) * SCORE_EXP2)
            m_ref[g] = top
            acc_ref[g] = acc_ref[g] * fade + dot(v, p.astype(BF16))

    def step(i_read, j_next, i, j, now, causal, begins):
        for g in range(NG):
            scores(i_read, j_next, 1 - now, [g])
            absorb(i, j, now, causal, begins, [g])

    def reset():
        m_ref[...] = jnp.full_like(m_ref, NEG)
        acc_ref[...] = jnp.zeros_like(acc_ref)

    def body(carry):
        i, j, slot = carry
        last = j == 2 * i + core
        i_next = jnp.where(last, i + 1, i)
        i_read = jnp.minimum(i_next, 3)
        j_next = jnp.where(last, meta_ref[0, i_read] // TK, j + 1)
        begins = j * TK < meta_ref[0, i]
        causal = last & jnp.logical_not(begins)

        @pl.when(last & (i < 3))
        def _():
            for n in range(2):
                prepare(2 * i + core + 1 + n)

        for now in range(2):
            turn = slot == now

            @pl.when(turn & begins)
            def _(now=now):
                step(i_read, j_next, i, j, now, True, True)

            @pl.when(turn & causal)
            def _(now=now):
                step(i_read, j_next, i, j, now, True, False)

            @pl.when(turn & jnp.logical_not(begins | causal))
            def _(now=now):
                step(i_read, j_next, i, j, now, False, False)

        @pl.when(last)
        def _():
            for g in range(NG):
                out = (acc_ref[g, :HD] * (1.0 / acc_ref[g, HD : HD + 1])).T.astype(BF16)
                for a in range(4):
                    low = (4 * (g % 2) + a) * HD
                    o_ref[g // 2, i, :, low : low + HD] = out[a * CHUNK : (a + 1) * CHUNK]
            pltpu.make_async_copy(o_ref.at[:, i], out_ref.at[:, i], o_sem.at[i]).start()
            reset()

        return (i_next, j_next, 1 - slot)

    reset()
    pltpu.make_async_copy(kv_ref, kv_ref, sem).wait()
    prepare(0)

    @pl.when(core == 1)
    def _():
        prepare(1)

    pltpu.make_async_copy(q_ref, q_ref, q_sem).wait()
    start = meta_ref[0, 0] // TK
    scores(0, start, 0, range(NG))
    lax.while_loop(lambda carry: carry[0] < 4, body, (jnp.int32(0), start, jnp.int32(0)))
    for n in range(4):
        pltpu.make_async_copy(o_ref.at[:, n], out_ref.at[:, n], o_sem.at[n]).wait()


def attend(meta, heads, own, other):
    return pl.pallas_call(
        attn_kernel,
        out_shape=jax.ShapeDtypeStruct((2, 4, CHUNK, 1024), BF16),
        in_specs=[SMEM] + [ANY] * 13,
        out_specs=ANY,
        scratch_shapes=[
            pltpu.VMEM((NG, 1, RG), F32),
            pltpu.VMEM((NG, HD + 16, RG), F32),
            pltpu.VMEM((NG, TK, RG), F32),
            pltpu.VMEM((NG, TK, RG), F32),
            pltpu.VMEM((8, CHUNK, 1024), BF16),
            pltpu.VMEM((4, 2, 4, 2, 2, CHUNK, 2 * HD), BF16),
            pltpu.VMEM((8, HD + 16, TK), BF16),
            pltpu.VMEM((2, 4, CHUNK, 1024), BF16),
            pltpu.SemaphoreType.DMA,
            pltpu.SemaphoreType.DMA,
            pltpu.SemaphoreType.DMA((4,)),
        ],
        compiler_params=pltpu.CompilerParams(vmem_limit_bytes=60 << 20),
        cost_estimate=pl.CostEstimate(
            flops=12_000_000_000, bytes_accessed=6 << 20, transcendentals=5_000_000
        ),
    )(meta, heads, *own, *other)


def one_minus_exp(u):
    small = -u * (
        1
        + u / 2 * (1 + u / 3 * (1 + u / 4 * (1 + u / 5 * (1 + u / 6 * (1 + u / 7 * (1 + u / 8))))))
    )
    return jnp.where(u > -0.5, small, 1 - jnp.exp(u))


def spread(columns, heads):
    rows = columns.shape[0]
    half = lax.broadcasted_iota(jnp.int32, (rows, 128), 1) // CHUNK
    parts = [
        jnp.take_along_axis(columns, half + h, axis=1, mode="promise_in_bounds")
        for h in range(0, heads, 2)
    ]
    return jnp.concatenate(parts, axis=1)


def running_decay(decay):
    row = lax.broadcasted_iota(jnp.int32, (CHUNK, CHUNK), 0)
    col = lax.broadcasted_iota(jnp.int32, (CHUNK, CHUNK), 1)
    tri = jnp.where(row >= col, 1.0, 0.0).astype(F32)
    return dot(tri, decay, precision=HIGHEST)


def own_columns(ref, place):
    block = ref[:, pl.ds(pl.multiple_of(place // 2 * 128, 128), 128)]
    return jnp.where(place % 2 == 1, block[:, CHUNK:], block[:, :CHUNK])


def state_kernel(place_ref, x_ref, dec_ref, b_ref, s_ref, f_ref, d_ref):
    decay = dec_ref[...].T[:CHUNK]
    run = running_decay(decay)
    drive = jnp.exp(run[CHUNK - 1 :] - run) * jnp.sqrt(one_minus_exp(2.0 * decay))
    end = jnp.exp(run[CHUNK - 1 :])
    high = end.astype(BF16).astype(F32)
    row = lax.broadcasted_iota(jnp.int32, (8, HM), 0)
    parts = jnp.where(row == 0, high, jnp.where(row == 1, end - high, 0.0))
    for k in range(16):
        f_ref[k, :, :16] = drive[:, 16 * k : 16 * k + 16]
        d_ref[k, :, :16] = parts[:, 16 * k : 16 * k + 16]
    b = own_columns(b_ref, place_ref[2])
    b_high = b.astype(BF16)
    b_low = (b - b_high.astype(F32)).astype(BF16)
    b_two = jnp.concatenate([b_high, b_low], axis=0)

    def block(k, carry):
        cols = pl.ds(pl.multiple_of(k * 1024, 1024), 1024)
        z = (x_ref[:, cols].astype(F32) * spread(f_ref[k], 16)).astype(BF16)
        two = dot(b_two, z)
        full = jnp.concatenate([two[:NS] + two[NS:], spread(d_ref[k], 16)], axis=0).astype(BF16)
        for m in range(8):
            s_ref[8 * k + m] = full[:, 128 * m : 128 * (m + 1)]
        return carry

    lax.fori_loop(0, 16, block, 0, unroll=4)


def chunk_states(place, x, dec, b):
    return pl.pallas_call(
        state_kernel,
        out_shape=jax.ShapeDtypeStruct((128, NS + 8, 128), BF16),
        in_specs=[SMEM] + [VMEM] * 3,
        out_specs=VMEM,
        scratch_shapes=[pltpu.VMEM((16, CHUNK, 128), F32), pltpu.VMEM((16, 8, 128), F32)],
        compiler_params=SMALL,
        cost_estimate=pl.CostEstimate(
            flops=30_000_000_000, bytes_accessed=3 << 20, transcendentals=50_000
        ),
    )(place, x, dec, b)


def output_kernel(place_ref, x_ref, dec_ref, b_ref, c_ref, e_ref, y_ref, f_ref, r_ref, g_ref):
    both = dec_ref[...].T
    decay = both[:CHUNK]
    run = running_decay(decay)
    drive = jnp.exp(-run) * jnp.sqrt(one_minus_exp(2.0 * decay))
    reach = jnp.exp(run)
    gain = jnp.broadcast_to(both[CHUNK : CHUNK + 1], (8, HM))
    for k in range(16):
        f_ref[k, :, :16] = drive[:, 16 * k : 16 * k + 16]
        r_ref[k, :, :16] = reach[:, 16 * k : 16 * k + 16]
        g_ref[k, :, :16] = gain[:, 16 * k : 16 * k + 16]
    row = lax.broadcasted_iota(jnp.int32, (CHUNK, CHUNK), 0)
    col = lax.broadcasted_iota(jnp.int32, (CHUNK, CHUNK), 1)
    b = own_columns(b_ref, place_ref[2])
    c = own_columns(c_ref, place_ref[2])
    inner = jnp.where(row >= col, dot(c, b, ((0,), (0,)), HIGHEST), 0.0)
    weights = jnp.concatenate([inner, c.T], axis=1).astype(BF16)

    def block(k, carry):
        cols = pl.ds(pl.multiple_of(k * 1024, 1024), 1024)
        x = x_ref[:, cols].astype(F32)
        z = (x * spread(f_ref[k], 16)).astype(BF16)
        entering = jnp.concatenate([e_ref[8 * k + m] for m in range(8)], axis=1)
        y = dot(weights, jnp.concatenate([z, entering], axis=0))
        y = y * spread(r_ref[k], 16) + spread(g_ref[k], 16)[:1] * x
        y_ref[:, cols] = y.astype(BF16)
        return carry

    lax.fori_loop(0, 16, block, 0, unroll=4)


def chunk_outputs(place, x, dec, b, c, entering):
    return pl.pallas_call(
        output_kernel,
        out_shape=jax.ShapeDtypeStruct((CHUNK, 16384), BF16),
        in_specs=[SMEM] + [VMEM] * 5,
        out_specs=VMEM,
        scratch_shapes=[
            pltpu.VMEM((16, CHUNK, 128), F32),
            pltpu.VMEM((16, CHUNK, 128), F32),
            pltpu.VMEM((16, 8, 128), F32),
        ],
        compiler_params=SMALL,
        cost_estimate=pl.CostEstimate(
            flops=2 * 80 * CHUNK * 16384, bytes_accessed=5 << 20, transcendentals=50_000
        ),
    )(place, x, dec, b, c, entering)


def enter_kernel(s_ref, e_ref):
    def chunk(k, state):
        e_ref[k] = state.astype(BF16)
        arrived = s_ref[k].astype(F32)
        return state * (arrived[NS : NS + 1] + arrived[NS + 1 : NS + 2]) + arrived[:NS]

    lax.fori_loop(0, 128, chunk, jnp.zeros((NS, 128), F32), unroll=8)


def entering_states(states):
    return pl.pallas_call(
        enter_kernel,
        out_shape=jax.ShapeDtypeStruct((128, NS, 128), BF16),
        in_specs=[VMEM],
        out_specs=VMEM,
        compiler_params=SMALL,
        cost_estimate=pl.CostEstimate(
            flops=60_000_000_000, bytes_accessed=2 << 20, transcendentals=0
        ),
    )(states)


def per_device(
    mamba_in, state_in_b, state_out_c, step_decay, skip_gain, queries, keys, values, doc_ids
):
    core, y, zh = lax.axis_index("core"), lax.axis_index("y"), lax.axis_index("zh")
    z = 2 * zh + lax.axis_index("zl")
    spot = jnp.stack([y, z, 4 * y + z]).astype(jnp.int32)
    b, c = state_in_b.T, state_out_c.T

    heads = lax.all_to_all(split_heads(queries, keys, values), HEADS, 0, 0, tiled=True)

    dec, heads = lax.optimization_barrier((split_decay(step_decay.T, skip_gain[None]), heads))
    dec = lax.all_to_all(dec, TP, 0, 0, tiled=True).reshape(HM, 2 * CHUNK)
    def along_z(block):
        return [block, lax.ppermute(block, "zh", [(0, 1), (1, 0)])]

    def along_y(block):
        steps = [[(n, (n + k) % 4) for n in range(4)] for k in range(1, 4)]
        return [block] + [lax.ppermute(block, "y", step) for step in steps]

    lead, tail = pick_kv(heads)
    lead, tail = stack(along_z(lead)), stack(along_y(tail))
    states = chunk_states(spot, mamba_in, dec, b)
    states, lead, tail = lax.optimization_barrier((states, lead, tail))
    own = along_y(lead) + along_z(tail)
    other = [lax.ppermute(block, "core", [(0, 1), (1, 0)]) for block in own]
    states = lax.all_to_all(states, ALL, 0, 0, tiled=True)

    blocks = jnp.arange(64)
    mine = (2 * jnp.arange(4)[:, None] + core) * 8 + 2 * y + zh
    doc = jnp.sum(jnp.where(blocks[None] == mine, doc_ids[None], 0), axis=1)
    first = jnp.sum(doc_ids[None] < doc[:, None], axis=1) * 128
    meta = jnp.stack([first, jnp.stack([core, y, zh, zh])]).astype(jnp.int32)
    entering = entering_states(states)
    entering, meta = lax.optimization_barrier((entering, meta))
    entering = lax.all_to_all(entering, ALL, 0, 0, tiled=True)
    attn = attend(meta, heads, own, other).reshape(8, CHUNK, 1024)
    attn = lax.all_to_all(attn, HEADS, 0, 0, tiled=True)
    mamba_out = chunk_outputs(spot, mamba_in, dec, b, c, entering)
    return (mamba_out, join_heads(attn))


def solution(mesh):
    inner = Mesh(mesh.devices.reshape(4, 2, 4, 2, 2), ALL)
    in_specs = (
        P(ALL, None),
        P(CTX, None),
        P(CTX, None),
        P(CTX, TP),
        P(TP),
        P(ALL, None),
        P(ALL, None),
        P(ALL, None),
        P(),
    )
    out_specs = (P(ALL, None), P(ALL, None))
    return jax.shard_map(
        per_device, mesh=inner, in_specs=in_specs, out_specs=out_specs, check_vma=False
    )
```
